32 devices in a mesh: rows: 8 (over y, x, core), cols: 4 (over z).
Axes of the slice: x: 2, y: 2, z: 4, core: 2. Of those that a mesh axis runs over, the one named last changes fastest.
Arguments:
- embeddings: bfloat16 [65536, 2048], P('rows', 'cols'), may hold values from -6 to 6
- pick_rows: int32 [2, 32], replicated, may hold values from 0 to 65535, as said below
Outputs:
- residual: float32 [65536, 2048], P('rows', 'cols')
The draws below stay inside these ranges and needn't reach their ends.
Inputs may be any that keep to these rules, and one draw needn't show every extreme that they name: `pick_rows`: all 64 indices are distinct; the picks of one round fall on the row owners as evenly as their count allows.
All inputs are finite; a program needn't handle non-finite values.
Results may differ from the reference program's by a relative error of at most 0.0003.
Values sent between devices are 32-bit elements; how exact they have to be, the bound alone decides.
A program may use at most 128 MiB of HBM per device.

```python
import jax
import jax.numpy as jnp
from jax import lax

W = 2048
ROWS_DEV = 8192
PICKS = 32
ROUNDS = 2
NROWS = 65536


def draw_pick_rows(key, part):
    key = jax.random.fold_in(key, 7)
    owners_total = NROWS // ROWS_DEV
    half_rows = ROWS_DEV // 2
    result_list = []
    for round_index in range(ROUNDS):
        round_key = jax.random.fold_in(key, round_index)
        owner_key, offset_key = jax.random.split(round_key)
        shift_value = jax.random.randint(owner_key, (), 0, owners_total)
        owner_ids = (jnp.arange(PICKS, dtype=jnp.int32) + shift_value) % owners_total
        slot_order = jnp.arange(PICKS, dtype=jnp.int32) // owners_total
        offset_table = jax.random.permutation(offset_key, half_rows).astype(jnp.int32)
        local_ids = jnp.take(offset_table, (slot_order + owner_ids * 7) % half_rows) + round_index * half_rows
        result_list.append(owner_ids * ROWS_DEV + local_ids)
    return jnp.stack(result_list, axis=0).astype(jnp.int32)


def block_scale(key, shape, cuts, low, largest):
    loudness = 1.0
    for position, parts in cuts:
        steps = jax.random.uniform(jax.random.fold_in(jax.random.fold_in(key, 6), position), (parts,), jnp.float32, low / len(cuts), largest / len(cuts))
        loudness = loudness * jnp.repeat(jnp.exp(steps), shape[position] // parts).reshape((-1,) + (1,) * (len(shape) - 1 - position))
    return loudness


def noise(own_key, dims, spread, most, cuts=(), kind=jnp.bfloat16):
    drawn = spread * jax.random.normal(own_key, dims, jnp.float32)
    if cuts:
        drawn = drawn * block_scale(own_key, dims, cuts, -0.22, 0.18)
    return jnp.clip(drawn, -most, most).astype(kind)


def setup_inputs(seed: int = 0) -> dict:
    streams_of = jax.random.split(jax.random.key(seed), 3)
    return {
        "embeddings": noise(streams_of[0], (NROWS, W), 1.0, 6.0, ((0, 8), (1, 4))),
        "pick_rows": draw_pick_rows(jax.random.fold_in(streams_of[2], 71), 0),
    }


def orthonormal_panel(pick_panel):
    gram_matrix = jnp.dot(pick_panel.astype(jnp.float32), pick_panel.T.astype(jnp.float32), precision=lax.Precision.HIGHEST, preferred_element_type=jnp.float32)
    factor = jnp.linalg.cholesky(gram_matrix)
    return jax.scipy.linalg.solve_triangular(factor, pick_panel, lower=True)

def reference(embeddings, pick_rows):
    residual = embeddings.astype(jnp.float32)
    for round_index in range(ROUNDS):
        pick_panel = jnp.take(residual, pick_rows[round_index], axis=0)
        basis_rows = orthonormal_panel(pick_panel)
        weights = jnp.dot(residual.astype(jnp.float32), basis_rows.T.astype(jnp.float32), precision=lax.Precision.HIGHEST, preferred_element_type=jnp.float32)
        residual = residual - jnp.dot(weights.astype(jnp.float32), basis_rows.astype(jnp.float32), precision=lax.Precision.HIGHEST, preferred_element_type=jnp.float32)
    return residual
```

```python
import functools

import jax
import jax.numpy as jnp
from jax import lax
from jax.experimental import pallas as pl
from jax.experimental.pallas import tpu as pltpu
from jax.sharding import PartitionSpec as P

HIGH = lax.Precision.HIGHEST
MESH = pl.DeviceIdType.MESH
GROUP = 16
CHUNKS = 32
LAG = 2
SOLVE_STEPS = 4
VMEM_LIMIT = 56 * 1024 * 1024


def own_picks_kernel(own_count, picks_ref, first_ref, emb_ref, out_ref, groups, offsets, sems):
    row_count = emb_ref.shape[0]
    total = picks_ref.shape[0]
    first = first_ref[0]

    def look(index, found):
        local = picks_ref[index] - first
        owned = (local >= 0) & (local < row_count) & (found < own_count)

        @pl.when(owned)
        def _():
            start = pl.multiple_of((local // GROUP) * GROUP, GROUP)
            offsets[found] = local - start
            pltpu.make_async_copy(
                emb_ref.at[pl.ds(start, GROUP), :], groups.at[found], sems.at[found]
            ).start()

        return found + owned.astype(jnp.int32)

    lax.fori_loop(0, total, look, jnp.int32(0))
    for slot in range(own_count):
        pltpu.make_async_copy(
            emb_ref.at[pl.ds(0, GROUP), :], groups.at[slot], sems.at[slot]
        ).wait()
        rows = groups[slot].astype(jnp.float32)
        inside = lax.broadcasted_iota(jnp.int32, rows.shape, 0) == offsets[slot]
        out_ref[pl.ds(slot, 1), :] = jnp.sum(jnp.where(inside, rows, 0.0), axis=0, keepdims=True)


def own_picks(embeddings, picks, first, own_count):
    width = embeddings.shape[1]
    return pl.pallas_call(
        functools.partial(own_picks_kernel, own_count),
        out_shape=jax.ShapeDtypeStruct((own_count, width), jnp.float32),
        in_specs=[
            pl.BlockSpec(memory_space=pltpu.SMEM),
            pl.BlockSpec(memory_space=pltpu.SMEM),
            pl.BlockSpec(memory_space=pl.ANY),
        ],
        out_specs=pl.BlockSpec(memory_space=pltpu.VMEM),
        scratch_shapes=[
            pltpu.VMEM((own_count, GROUP, width), embeddings.dtype),
            pltpu.SMEM((own_count,), jnp.int32),
            pltpu.SemaphoreType.DMA((own_count,)),
        ],
    )(picks, first, embeddings)


def weights_kernel(
    rows_n, cols_n, chunks, emb_ref, own_ref, weights_ref, panels_ref,
    emb, gathered, panel_t, system, mine, from_left, from_right, to_right, to_left,
    emb_sem, row_send, row_recv, right_send, left_recv, left_send, right_recv,
):
    own_count, width = own_ref.shape
    rank = rows_n * own_count
    half = rank // 2
    size = weights_ref.shape[0] // chunks
    row = lax.axis_index("rows")
    col = lax.axis_index("cols")
    has_left = col > 0
    has_right = col < cols_n - 1

    load = pltpu.make_async_copy(emb_ref, emb, emb_sem)
    load.start()

    barrier = pltpu.get_barrier_semaphore()
    for step in range(1, rows_n):
        pl.semaphore_signal(
            barrier, inc=1, device_id={"rows": lax.rem(row + step, rows_n)}, device_id_type=MESH
        )

    @pl.when(has_left)
    def _():
        pl.semaphore_signal(barrier, inc=1, device_id={"cols": col - 1}, device_id_type=MESH)

    @pl.when(has_right)
    def _():
        pl.semaphore_signal(barrier, inc=1, device_id={"cols": col + 1}, device_id_type=MESH)

    @pl.when(jnp.logical_not(has_left))
    def _():
        from_left[...] = jnp.zeros_like(from_left)

    @pl.when(jnp.logical_not(has_right))
    def _():
        from_right[...] = jnp.zeros_like(from_right)

    pl.semaphore_wait(
        barrier, rows_n - 1 + has_left.astype(jnp.int32) + has_right.astype(jnp.int32)
    )

    def row_copy(step):
        return pltpu.make_async_remote_copy(
            src_ref=own_ref,
            dst_ref=gathered.at[row],
            send_sem=row_send.at[step],
            recv_sem=row_recv.at[row],
            device_id={"rows": lax.rem(row + step, rows_n)},
            device_id_type=MESH,
        )

    for step in range(1, rows_n):
        row_copy(step).start()
    gathered[row] = own_ref[...]
    mine[pl.ds(0, size), :] = jnp.zeros((size, 2 * rank), jnp.float32)
    for step in range(1, rows_n):
        source = lax.rem(row + step, rows_n)
        pltpu.make_async_remote_copy(
            src_ref=own_ref,
            dst_ref=gathered.at[source],
            send_sem=row_send.at[step],
            recv_sem=row_recv.at[source],
            device_id={"rows": source},
            device_id_type=MESH,
        ).wait_recv()

    panel = jnp.concatenate([gathered[owner] for owner in range(rows_n)], axis=0)
    panel16 = panel.astype(jnp.bfloat16)
    nothing = jnp.zeros_like(panel)
    for side in range(2):
        padded = jnp.concatenate([panel, nothing] if side == 0 else [nothing, panel], axis=0)
        panel_t[side] = padded.T.astype(jnp.bfloat16)
        for piece in range(3):
            panels_ref[side, pl.ds(piece * 2 * rank, 2 * rank), :] = padded.astype(jnp.bfloat16)

    mine[pl.ds(0, half), :] = jnp.dot(
        panel16[:half], panel_t[0], preferred_element_type=jnp.float32
    ) + jnp.dot(panel16[half:], panel_t[1], preferred_element_type=jnp.float32)

    def part(index):
        return pl.ds(pl.multiple_of(index * size, size), size)

    def right_copy(index):
        return pltpu.make_async_remote_copy(
            src_ref=to_right.at[part(index)],
            dst_ref=from_left.at[part(index)],
            send_sem=right_send.at[index],
            recv_sem=left_recv.at[index],
            device_id={"cols": lax.rem(col + 1, cols_n)},
            device_id_type=MESH,
        )

    def left_copy(index):
        return pltpu.make_async_remote_copy(
            src_ref=to_left.at[part(index)],
            dst_ref=from_right.at[part(index)],
            send_sem=left_send.at[index],
            recv_sem=right_recv.at[index],
            device_id={"cols": lax.rem(col + cols_n - 1, cols_n)},
            device_id_type=MESH,
        )

    parts = chunks + 1
    hops = (cols_n - 1) * LAG
    solve_from = hops + 1
    solve_turns = rank // SOLVE_STEPS
    weigh_from = solve_from + solve_turns
    turns = parts + hops
    lanes = lax.broadcasted_iota(jnp.int32, (rank, 2 * rank), 1)
    sublanes = lax.broadcasted_iota(jnp.int32, (rank, 2 * rank), 0)
    load.wait()

    def summed(index):
        return mine[part(index), :] + from_left[part(index), :] + from_right[part(index), :]

    def eliminate(step, _):
        now = system[0:rank, :]
        picked = system[pl.ds(step, 1), :]
        on_lane = lanes == step
        on_row = sublanes == step
        column = jnp.sum(jnp.where(on_lane, now, 0.0), axis=1, keepdims=True)
        pivot = jnp.sum(jnp.where(on_lane[0:1], picked, 0.0), axis=1, keepdims=True)
        new_row = jnp.where(on_lane[0:1], 1.0, picked) / pivot
        rest = jnp.where(on_lane, 0.0, now) - column * new_row
        system[0:rank, :] = jnp.where(on_row, jnp.broadcast_to(new_row, now.shape), rest)
        return 0

    def weigh(index):
        at = pl.ds(pl.multiple_of((index - 1) * size, size), size)
        weights_ref[at, :] = jnp.dot(
            summed(index), system[...], precision=HIGH, preferred_element_type=jnp.float32
        )

    def turn(index, _):
        @pl.when((index >= 1) & (index < parts))
        def _():
            at = pl.ds(pl.multiple_of((index - 1) * size, size), size)
            mine[part(index), :] = jnp.dot(
                emb[0, at, :], panel_t[0], preferred_element_type=jnp.float32
            ) + jnp.dot(emb[1, at, :], panel_t[1], preferred_element_type=jnp.float32)

        left_index = index - col * LAG
        right_index = index - (cols_n - 1 - col) * LAG

        @pl.when((left_index >= 0) & (left_index < parts))
        def _():
            @pl.when(has_left)
            def _():
                right_copy(left_index).wait_recv()

            @pl.when(has_right)
            def _():
                to_right[part(left_index), :] = (
                    mine[part(left_index), :] + from_left[part(left_index), :]
                )
                right_copy(left_index).start()

        @pl.when((right_index >= 0) & (right_index < parts))
        def _():
            @pl.when(has_right)
            def _():
                left_copy(right_index).wait_recv()

            @pl.when(has_left)
            def _():
                to_left[part(right_index), :] = (
                    mine[part(right_index), :] + from_right[part(right_index), :]
                )
                left_copy(right_index).start()

        @pl.when(index == hops)
        def _():
            at = pl.ds(0, half)
            packed = mine[at, :] + from_left[at, :] + from_right[at, :]
            inside = lanes[0:half] < rank
            system[0:half, :] = jnp.where(inside, packed, 0.0)
            system[half:rank, :] = jnp.where(inside, pltpu.roll(packed, rank, 1), 0.0)

        @pl.when((index >= solve_from) & (index < weigh_from))
        def _():
            lax.fori_loop(
                (index - solve_from) * SOLVE_STEPS,
                (index - solve_from + 1) * SOLVE_STEPS,
                eliminate,
                0,
            )

        @pl.when(index == weigh_from)
        def _():
            system[rank : 2 * rank, :] = pltpu.roll(system[0:rank, :], rank, 1)

        @pl.when(index >= weigh_from)
        def _():
            weigh((index - weigh_from) * 2 + 1)
            weigh((index - weigh_from) * 2 + 2)

        return 0

    lax.fori_loop(0, turns, turn, 0)
    weighed = (turns - weigh_from) * 2

    def finish(index, _):
        weigh(index)
        return 0

    lax.fori_loop(weighed + 1, parts, finish, 0)

    for step in range(1, rows_n):
        row_copy(step).wait_send()

    def sent(index, _):
        @pl.when(has_right)
        def _():
            right_copy(index).wait_send()

        @pl.when(has_left)
        def _():
            left_copy(index).wait_send()

        return 0

    lax.fori_loop(0, parts, sent, 0)


def all_weights(emb3, own, rows_n, cols_n, rank):
    _, pairs, width = emb3.shape
    size = pairs // CHUNKS
    buffer = pltpu.VMEM((pairs + size, 2 * rank), jnp.float32)
    dma = pltpu.SemaphoreType.DMA
    return pl.pallas_call(
        functools.partial(weights_kernel, rows_n, cols_n, CHUNKS),
        out_shape=(
            jax.ShapeDtypeStruct((pairs, 2 * rank), jnp.float32),
            jax.ShapeDtypeStruct((2, 6 * rank, width), jnp.bfloat16),
        ),
        in_specs=[pl.BlockSpec(memory_space=pl.ANY), pl.BlockSpec(memory_space=pltpu.VMEM)],
        out_specs=(
            pl.BlockSpec(memory_space=pltpu.VMEM),
            pl.BlockSpec(memory_space=pltpu.VMEM),
        ),
        scratch_shapes=[
            pltpu.VMEM(emb3.shape, emb3.dtype),
            pltpu.VMEM((rows_n,) + own.shape, jnp.float32),
            pltpu.VMEM((2, width, 2 * rank), jnp.bfloat16),
            pltpu.VMEM((2 * rank, 2 * rank), jnp.float32),
            buffer, buffer, buffer, buffer, buffer,
            dma, dma((rows_n,)), dma((rows_n,)),
            dma((CHUNKS + 1,)), dma((CHUNKS + 1,)), dma((CHUNKS + 1,)), dma((CHUNKS + 1,)),
        ],
        compiler_params=pltpu.CompilerParams(
            collective_id=0, has_side_effects=True, vmem_limit_bytes=VMEM_LIMIT
        ),
        cost_estimate=pl.CostEstimate(
            flops=8 * pairs * width * rank, bytes_accessed=2 * emb3.size, transcendentals=0
        ),
    )(emb3, own)


def subtract_kernel(emb_ref, weights_ref, panels_ref, out_ref):
    weights = weights_ref[...]
    first = weights.astype(jnp.bfloat16)
    rest = weights - first.astype(jnp.float32)
    second = rest.astype(jnp.bfloat16)
    third = (rest - second.astype(jnp.float32)).astype(jnp.bfloat16)
    pieces = jnp.concatenate([first, second, third], axis=1)
    for side in range(2):
        out_ref[side] = emb_ref[side].astype(jnp.float32) - jnp.dot(
            pieces, panels_ref[side], preferred_element_type=jnp.float32
        )


def subtract(emb3, weights, panels):
    _, pairs, width = emb3.shape
    block = min(512, pairs)
    return pl.pallas_call(
        subtract_kernel,
        grid=(pairs // block,),
        out_shape=jax.ShapeDtypeStruct(emb3.shape, jnp.float32),
        in_specs=[
            pl.BlockSpec((2, block, width), lambda i: (0, i, 0)),
            pl.BlockSpec((block, weights.shape[1]), lambda i: (i, 0)),
            pl.BlockSpec(panels.shape, lambda i: (0, 0, 0)),
        ],
        out_specs=pl.BlockSpec((2, block, width), lambda i: (0, i, 0)),
        compiler_params=pltpu.CompilerParams(vmem_limit_bytes=VMEM_LIMIT),
    )(emb3, weights, panels)


def per_device(rows_n, cols_n, embeddings, pick_rows):
    row_count, width = embeddings.shape
    rank = pick_rows.shape[0] * pick_rows.shape[1]
    first = (lax.axis_index("rows") * row_count).astype(jnp.int32).reshape(1)
    own = own_picks(embeddings, pick_rows.reshape(rank), first, rank // rows_n)
    emb3 = embeddings.reshape(2, row_count // 2, width)
    weights, panels = all_weights(emb3, own, rows_n, cols_n, rank)
    return subtract(emb3, weights, panels).reshape(row_count, width)


def solution(mesh):
    in_specs = (P("rows", "cols"), P())
    out_specs = P("rows", "cols")
    return jax.shard_map(
        functools.partial(per_device, mesh.shape["rows"], mesh.shape["cols"]),
        mesh=mesh, in_specs=in_specs, out_specs=out_specs, check_vma=False,
    )
```

```python
import functools

import jax
import jax.numpy as jnp
from jax import lax
from jax.experimental import pallas as pl
from jax.experimental.pallas import tpu as pltpu
from jax.sharding import PartitionSpec as P

HIGH = lax.Precision.HIGHEST
MESH = pl.DeviceIdType.MESH
GROUP = 16
CHUNKS = 32
LAG = 4
BLOCK_PARTS = 4
SOLVE_STEPS = 4
MIB = 1024 * 1024


def own_picks_kernel(own_count, picks_ref, emb_ref, out_ref, groups, offsets, sems):
    row_count = emb_ref.shape[0]
    rounds, per_round = picks_ref.shape
    first = lax.axis_index("rows") * row_count

    def look(index, found):
        local = picks_ref[index // per_round, index % per_round] - first
        owned = (local >= 0) & (local < row_count) & (found < own_count)

        @pl.when(owned)
        def _():
            start = pl.multiple_of((local // GROUP) * GROUP, GROUP)
            offsets[found] = local - start
            pltpu.make_async_copy(
                emb_ref.at[pl.ds(start, GROUP), :], groups.at[found], sems.at[found]
            ).start()

        return found + owned.astype(jnp.int32)

    lax.fori_loop(0, rounds * per_round, look, jnp.int32(0), unroll=8)
    for slot in range(own_count):
        pltpu.make_async_copy(
            emb_ref.at[pl.ds(0, GROUP), :], groups.at[slot], sems.at[slot]
        ).wait()
        rows = groups[slot].astype(jnp.float32)
        inside = lax.broadcasted_iota(jnp.int32, rows.shape, 0) == offsets[slot]
        out_ref[pl.ds(slot, 1), :] = jnp.sum(jnp.where(inside, rows, 0.0), axis=0, keepdims=True)


def own_picks(embeddings, picks, own_count):
    width = embeddings.shape[1]
    return pl.pallas_call(
        functools.partial(own_picks_kernel, own_count),
        out_shape=jax.ShapeDtypeStruct((own_count, width), jnp.float32),
        in_specs=[
            pl.BlockSpec(memory_space=pltpu.SMEM),
            pl.BlockSpec(memory_space=pl.ANY),
        ],
        out_specs=pl.BlockSpec(memory_space=pltpu.VMEM),
        scratch_shapes=[
            pltpu.VMEM((own_count, GROUP, width), embeddings.dtype),
            pltpu.SMEM((own_count,), jnp.int32),
            pltpu.SemaphoreType.DMA((own_count,)),
        ],
        compiler_params=pltpu.CompilerParams(vmem_limit_bytes=60 * MIB),
    )(picks, embeddings)


def weights_kernel(
    rows_n, cols_n, chunks, emb_ref, own_ref, weights_ref, panels_ref,
    emb, gathered, panel_t, system, mine, from_left, from_right, to_right, to_left,
    emb_sem, row_send, row_recv, right_send, left_recv, left_send, right_recv,
):
    own_count, width = own_ref.shape
    rank = rows_n * own_count
    half = rank // 2
    size = weights_ref.shape[0] // chunks
    row = lax.axis_index("rows")
    col = lax.axis_index("cols")
    has_left = col > 0
    has_right = col < cols_n - 1

    load = pltpu.make_async_copy(emb_ref, emb, emb_sem)
    load.start()

    barrier = pltpu.get_barrier_semaphore()
    for step in range(1, rows_n):
        pl.semaphore_signal(
            barrier, inc=1, device_id={"rows": lax.rem(row + step, rows_n)}, device_id_type=MESH
        )

    @pl.when(has_left)
    def _():
        pl.semaphore_signal(barrier, inc=1, device_id={"cols": col - 1}, device_id_type=MESH)

    @pl.when(has_right)
    def _():
        pl.semaphore_signal(barrier, inc=1, device_id={"cols": col + 1}, device_id_type=MESH)

    @pl.when(jnp.logical_not(has_left))
    def _():
        from_left[...] = jnp.zeros_like(from_left)

    @pl.when(jnp.logical_not(has_right))
    def _():
        from_right[...] = jnp.zeros_like(from_right)

    pl.semaphore_wait(
        barrier, rows_n - 1 + has_left.astype(jnp.int32) + has_right.astype(jnp.int32)
    )

    def row_copy(step):
        return pltpu.make_async_remote_copy(
            src_ref=own_ref,
            dst_ref=gathered.at[row],
            send_sem=row_send.at[step],
            recv_sem=row_recv.at[row],
            device_id={"rows": lax.rem(row + step, rows_n)},
            device_id_type=MESH,
        )

    for step in range(1, rows_n):
        row_copy(step).start()
    gathered[row] = own_ref[...]
    mine[pl.ds(0, size), :] = jnp.zeros((size, 2 * rank), jnp.float32)
    for step in range(1, rows_n):
        source = lax.rem(row + step, rows_n)
        pltpu.make_async_remote_copy(
            src_ref=own_ref,
            dst_ref=gathered.at[source],
            send_sem=row_send.at[step],
            recv_sem=row_recv.at[source],
            device_id={"rows": source},
            device_id_type=MESH,
        ).wait_recv()

    panel = jnp.concatenate([gathered[owner] for owner in range(rows_n)], axis=0)
    panel16 = panel.astype(jnp.bfloat16)
    nothing = jnp.zeros_like(panel)
    for side in range(2):
        padded = jnp.concatenate([panel, nothing] if side == 0 else [nothing, panel], axis=0)
        panel_t[side] = padded.T.astype(jnp.bfloat16)
        for piece in range(3):
            panels_ref[side, pl.ds(piece * 2 * rank, 2 * rank), :] = padded.astype(jnp.bfloat16)

    mine[pl.ds(0, half), :] = jnp.dot(
        panel16[:half], panel_t[0], preferred_element_type=jnp.float32
    ) + jnp.dot(panel16[half:], panel_t[1], preferred_element_type=jnp.float32)

    def part(index):
        return pl.ds(pl.multiple_of(index * size, size), size)

    def right_copy(index):
        return pltpu.make_async_remote_copy(
            src_ref=to_right.at[part(index)],
            dst_ref=from_left.at[part(index)],
            send_sem=right_send.at[index],
            recv_sem=left_recv.at[index],
            device_id={"cols": lax.rem(col + 1, cols_n)},
            device_id_type=MESH,
        )

    def left_copy(index):
        return pltpu.make_async_remote_copy(
            src_ref=to_left.at[part(index)],
            dst_ref=from_right.at[part(index)],
            send_sem=left_send.at[index],
            recv_sem=right_recv.at[index],
            device_id={"cols": lax.rem(col + cols_n - 1, cols_n)},
            device_id_type=MESH,
        )

    parts = chunks + 1
    hops = (cols_n - 1) * LAG
    solve_from = hops + 1
    solve_turns = rank // SOLVE_STEPS
    weigh_from = solve_from + solve_turns
    turns = parts + hops
    assert turns + 1 - 2 * (chunks // BLOCK_PARTS) >= weigh_from
    lanes = lax.broadcasted_iota(jnp.int32, (rank, 2 * rank), 1)
    sublanes = lax.broadcasted_iota(jnp.int32, (rank, 2 * rank), 0)
    load.wait()

    def eliminate(step, _):
        now = system[0:rank, :]
        picked = system[pl.ds(step, 1), :]
        on_lane = lanes == step
        on_row = sublanes == step
        column = jnp.sum(jnp.where(on_lane, now, 0.0), axis=1, keepdims=True)
        pivot = jnp.sum(jnp.where(on_lane[0:1], picked, 0.0), axis=1, keepdims=True)
        new_row = jnp.where(on_lane[0:1], 1.0, picked) / pivot
        rest = jnp.where(on_lane, 0.0, now) - column * new_row
        system[0:rank, :] = jnp.where(on_row, jnp.broadcast_to(new_row, now.shape), rest)
        return 0

    block = BLOCK_PARTS * size
    blocks = chunks // BLOCK_PARTS

    def block_rows(index):
        start = pl.multiple_of(index * block, block)
        return pl.ds(start, block), pl.ds(pl.multiple_of(start + size, size), block)

    def multiply(index):
        at, kept = block_rows(index)
        mine[kept, :] = jnp.dot(
            emb[0, at, :], panel_t[0], preferred_element_type=jnp.float32
        ) + jnp.dot(emb[1, at, :], panel_t[1], preferred_element_type=jnp.float32)

    def weigh(index):
        at, kept = block_rows(index)
        total = mine[kept, :] + from_left[kept, :] + from_right[kept, :]
        weights_ref[at, :] = jnp.dot(
            total, system[...], precision=HIGH, preferred_element_type=jnp.float32
        )

    multiply(0)

    def turn(index, _):
        @pl.when((index % BLOCK_PARTS == 1) & (index < chunks - BLOCK_PARTS))
        def _():
            multiply(index // BLOCK_PARTS + 1)

        left_index = index - col * LAG
        right_index = index - (cols_n - 1 - col) * LAG

        @pl.when((left_index >= 0) & (left_index < parts))
        def _():
            @pl.when(has_left)
            def _():
                right_copy(left_index).wait_recv()

            @pl.when(has_right)
            def _():
                to_right[part(left_index), :] = (
                    mine[part(left_index), :] + from_left[part(left_index), :]
                )
                right_copy(left_index).start()

        @pl.when((right_index >= 0) & (right_index < parts))
        def _():
            @pl.when(has_right)
            def _():
                left_copy(right_index).wait_recv()

            @pl.when(has_left)
            def _():
                to_left[part(right_index), :] = (
                    mine[part(right_index), :] + from_right[part(right_index), :]
                )
                left_copy(right_index).start()

        @pl.when(index == hops)
        def _():
            at = pl.ds(0, half)
            packed = mine[at, :] + from_left[at, :] + from_right[at, :]
            inside = lanes[0:half] < rank
            system[0:half, :] = jnp.where(inside, packed, 0.0)
            system[half:rank, :] = jnp.where(inside, pltpu.roll(packed, rank, 1), 0.0)

        @pl.when((index >= solve_from) & (index < weigh_from))
        def _():
            lax.fori_loop(
                (index - solve_from) * SOLVE_STEPS,
                (index - solve_from + 1) * SOLVE_STEPS,
                eliminate,
                0,
            )

        @pl.when(index == weigh_from)
        def _():
            system[rank : 2 * rank, :] = pltpu.roll(system[0:rank, :], rank, 1)

        since = index - (turns + 1 - 2 * blocks)

        @pl.when((since >= 0) & (since % 2 == 0))
        def _():
            weigh(since // 2)

        return 0

    lax.fori_loop(0, turns, turn, 0)

    for step in range(1, rows_n):
        row_copy(step).wait_send()

    def sent(index, _):
        @pl.when(has_right)
        def _():
            right_copy(index).wait_send()

        @pl.when(has_left)
        def _():
            left_copy(index).wait_send()

        return 0

    lax.fori_loop(0, parts, sent, 0)


def all_weights(emb3, own, rows_n, cols_n, rank):
    _, pairs, width = emb3.shape
    size = pairs // CHUNKS
    buffer = pltpu.VMEM((pairs + size, 2 * rank), jnp.float32)
    dma = pltpu.SemaphoreType.DMA
    return pl.pallas_call(
        functools.partial(weights_kernel, rows_n, cols_n, CHUNKS),
        out_shape=(
            jax.ShapeDtypeStruct((pairs, 2 * rank), jnp.float32),
            jax.ShapeDtypeStruct((2, 6 * rank, width), jnp.bfloat16),
        ),
        in_specs=[pl.BlockSpec(memory_space=pl.ANY), pl.BlockSpec(memory_space=pltpu.VMEM)],
        out_specs=(
            pl.BlockSpec(memory_space=pltpu.VMEM),
            pl.BlockSpec(memory_space=pltpu.VMEM),
        ),
        scratch_shapes=[
            pltpu.VMEM(emb3.shape, emb3.dtype),
            pltpu.VMEM((rows_n,) + own.shape, jnp.float32),
            pltpu.VMEM((2, width, 2 * rank), jnp.bfloat16),
            pltpu.VMEM((2 * rank, 2 * rank), jnp.float32),
            buffer, buffer, buffer, buffer, buffer,
            dma, dma((rows_n,)), dma((rows_n,)),
            dma((CHUNKS + 1,)), dma((CHUNKS + 1,)), dma((CHUNKS + 1,)), dma((CHUNKS + 1,)),
        ],
        compiler_params=pltpu.CompilerParams(
            collective_id=0, has_side_effects=True, vmem_limit_bytes=28 * MIB
        ),
        cost_estimate=pl.CostEstimate(
            flops=8 * pairs * width * rank, bytes_accessed=2 * emb3.size, transcendentals=0
        ),
    )(emb3, own)


def subtract_kernel(emb_ref, weights_ref, panels_ref, out_ref):
    weights = weights_ref[...]
    first = weights.astype(jnp.bfloat16)
    rest = weights - first.astype(jnp.float32)
    second = rest.astype(jnp.bfloat16)
    third = (rest - second.astype(jnp.float32)).astype(jnp.bfloat16)
    pieces = jnp.concatenate([first, second, third], axis=1)
    for side in range(2):
        out_ref[side] = emb_ref[side].astype(jnp.float32) - jnp.dot(
            pieces, panels_ref[side], preferred_element_type=jnp.float32
        )


def subtract(emb3, weights, panels):
    _, pairs, width = emb3.shape
    block = min(512, pairs)
    return pl.pallas_call(
        subtract_kernel,
        grid=(pairs // block,),
        out_shape=jax.ShapeDtypeStruct(emb3.shape, jnp.float32),
        in_specs=[
            pl.BlockSpec((2, block, width), lambda i: (0, i, 0)),
            pl.BlockSpec((block, weights.shape[1]), lambda i: (i, 0)),
            pl.BlockSpec(panels.shape, lambda i: (0, 0, 0)),
        ],
        out_specs=pl.BlockSpec((2, block, width), lambda i: (0, i, 0)),
        compiler_params=pltpu.CompilerParams(vmem_limit_bytes=16 * MIB),
    )(emb3, weights, panels)


def per_device(rows_n, cols_n, embeddings, pick_rows):
    row_count, width = embeddings.shape
    rank = pick_rows.shape[0] * pick_rows.shape[1]
    own = own_picks(embeddings, pick_rows, rank // rows_n)
    emb3 = embeddings.reshape(2, row_count // 2, width)
    weights, panels = all_weights(emb3, own, rows_n, cols_n, rank)
    return subtract(emb3, weights, panels).reshape(row_count, width)


def solution(mesh):
    in_specs = (P("rows", "cols"), P())
    out_specs = P("rows", "cols")
    return jax.shard_map(
        functools.partial(per_device, mesh.shape["rows"], mesh.shape["cols"]),
        mesh=mesh, in_specs=in_specs, out_specs=out_specs, check_vma=False,
    )
```

```python
import functools

import jax
import jax.numpy as jnp
from jax import lax
from jax.experimental import pallas as pl
from jax.experimental.pallas import tpu as pltpu
from jax.sharding import PartitionSpec as P

HIGH = lax.Precision.HIGHEST
MESH = pl.DeviceIdType.MESH
GROUP = 16
CHUNKS = 32
LAG = 4
BLOCK_PARTS = 4
SOLVE_STEPS = 4
MIB = 1024 * 1024


def own_picks_kernel(own_count, picks_ref, emb_ref, out_ref, groups, offsets, sems):
    row_count = emb_ref.shape[0]
    rounds, per_round = picks_ref.shape
    first = lax.axis_index("rows") * row_count

    def look(index, found):
        local = picks_ref[index // per_round, index % per_round] - first
        owned = (local >= 0) & (local < row_count) & (found < own_count)

        @pl.when(owned)
        def _():
            start = pl.multiple_of((local // GROUP) * GROUP, GROUP)
            offsets[found] = local - start
            pltpu.make_async_copy(
                emb_ref.at[pl.ds(start, GROUP), :], groups.at[found], sems.at[found]
            ).start()

        return found + owned.astype(jnp.int32)

    lax.fori_loop(0, rounds * per_round, look, jnp.int32(0), unroll=8)
    for slot in range(own_count):
        pltpu.make_async_copy(
            emb_ref.at[pl.ds(0, GROUP), :], groups.at[slot], sems.at[slot]
        ).wait()
        rows = groups[slot].astype(jnp.float32)
        inside = lax.broadcasted_iota(jnp.int32, rows.shape, 0) == offsets[slot]
        out_ref[pl.ds(slot, 1), :] = jnp.sum(jnp.where(inside, rows, 0.0), axis=0, keepdims=True)


def own_picks(embeddings, picks, own_count):
    width = embeddings.shape[1]
    return pl.pallas_call(
        functools.partial(own_picks_kernel, own_count),
        out_shape=jax.ShapeDtypeStruct((own_count, width), jnp.float32),
        in_specs=[
            pl.BlockSpec(memory_space=pltpu.SMEM),
            pl.BlockSpec(memory_space=pl.ANY),
        ],
        out_specs=pl.BlockSpec(memory_space=pltpu.VMEM),
        scratch_shapes=[
            pltpu.VMEM((own_count, GROUP, width), embeddings.dtype),
            pltpu.SMEM((own_count,), jnp.int32),
            pltpu.SemaphoreType.DMA((own_count,)),
        ],
        compiler_params=pltpu.CompilerParams(vmem_limit_bytes=52 * MIB),
    )(picks, embeddings)


def weights_kernel(
    rows_n, cols_n, chunks, emb_ref, own_ref, emb, weights_ref, panels_ref,
    gathered, panel_t, system, mine, from_left, from_right, to_right, to_left,
    emb_sem, row_send, row_recv, right_send, left_recv, left_send, right_recv,
):
    own_count, width = own_ref.shape
    rank = rows_n * own_count
    half = rank // 2
    size = weights_ref.shape[0] // chunks
    row = lax.axis_index("rows")
    col = lax.axis_index("cols")
    has_left = col > 0
    has_right = col < cols_n - 1

    load = pltpu.make_async_copy(emb_ref, emb, emb_sem)
    load.start()

    barrier = pltpu.get_barrier_semaphore()
    for step in range(1, rows_n):
        pl.semaphore_signal(
            barrier, inc=1, device_id={"rows": lax.rem(row + step, rows_n)}, device_id_type=MESH
        )

    @pl.when(has_left)
    def _():
        pl.semaphore_signal(barrier, inc=1, device_id={"cols": col - 1}, device_id_type=MESH)

    @pl.when(has_right)
    def _():
        pl.semaphore_signal(barrier, inc=1, device_id={"cols": col + 1}, device_id_type=MESH)

    @pl.when(jnp.logical_not(has_left))
    def _():
        from_left[...] = jnp.zeros_like(from_left)

    @pl.when(jnp.logical_not(has_right))
    def _():
        from_right[...] = jnp.zeros_like(from_right)

    pl.semaphore_wait(
        barrier, rows_n - 1 + has_left.astype(jnp.int32) + has_right.astype(jnp.int32)
    )

    def row_copy(step):
        return pltpu.make_async_remote_copy(
            src_ref=own_ref,
            dst_ref=gathered.at[row],
            send_sem=row_send.at[step],
            recv_sem=row_recv.at[row],
            device_id={"rows": lax.rem(row + step, rows_n)},
            device_id_type=MESH,
        )

    for step in range(1, rows_n):
        row_copy(step).start()
    gathered[row] = own_ref[...]
    for step in range(1, rows_n):
        source = lax.rem(row + step, rows_n)
        pltpu.make_async_remote_copy(
            src_ref=own_ref,
            dst_ref=gathered.at[source],
            send_sem=row_send.at[step],
            recv_sem=row_recv.at[source],
            device_id={"rows": source},
            device_id_type=MESH,
        ).wait_recv()

    def padded_panel(side):
        panel = jnp.concatenate([gathered[owner] for owner in range(rows_n)], axis=0)
        nothing = jnp.zeros_like(panel)
        return jnp.concatenate([panel, nothing] if side == 0 else [nothing, panel], axis=0)

    for side in range(2):
        panel_t[side] = padded_panel(side).T.astype(jnp.bfloat16)
    panel16 = padded_panel(0)[:rank].astype(jnp.bfloat16)

    mine[pl.ds(0, half), :] = jnp.dot(
        panel16[:half], panel_t[0], preferred_element_type=jnp.float32
    ) + jnp.dot(panel16[half:], panel_t[1], preferred_element_type=jnp.float32)

    def part(index):
        return pl.ds(pl.multiple_of(index * size, size), size)

    def right_copy(index, at):
        return pltpu.make_async_remote_copy(
            src_ref=to_right.at[at],
            dst_ref=from_left.at[at],
            send_sem=right_send.at[index],
            recv_sem=left_recv.at[index],
            device_id={"cols": lax.rem(col + 1, cols_n)},
            device_id_type=MESH,
        )

    def left_copy(index, at):
        return pltpu.make_async_remote_copy(
            src_ref=to_left.at[at],
            dst_ref=from_right.at[at],
            send_sem=left_send.at[index],
            recv_sem=right_recv.at[index],
            device_id={"cols": lax.rem(col + cols_n - 1, cols_n)},
            device_id_type=MESH,
        )

    parts = chunks + 1
    hops = (cols_n - 1) * LAG
    solve_from = hops + 1
    solve_turns = rank // SOLVE_STEPS
    weigh_from = solve_from + solve_turns
    turns = parts + hops
    assert turns + 1 - 2 * (chunks // BLOCK_PARTS) >= weigh_from
    lanes = lax.broadcasted_iota(jnp.int32, (rank, 2 * rank), 1)
    sublanes = lax.broadcasted_iota(jnp.int32, (rank, 2 * rank), 0)

    def eliminate(step, _):
        now = system[0:rank, :]
        picked = system[pl.ds(step, 1), :]
        on_lane = lanes == step
        on_row = sublanes == step
        column = jnp.sum(jnp.where(on_lane, now, 0.0), axis=1, keepdims=True)
        pivot = jnp.sum(jnp.where(on_lane[0:1], picked, 0.0), axis=1, keepdims=True)
        new_row = jnp.where(on_lane[0:1], 1.0, picked) / pivot
        rest = jnp.where(on_lane, 0.0, now) - column * new_row
        system[0:rank, :] = jnp.where(on_row, jnp.broadcast_to(new_row, now.shape), rest)
        return 0

    block = BLOCK_PARTS * size
    blocks = chunks // BLOCK_PARTS

    def block_rows(index):
        start = pl.multiple_of(index * block, block)
        return pl.ds(start, block), pl.ds(pl.multiple_of(start + size, size), block)

    def multiply(index):
        @pl.when(index == 0)
        def _():
            load.wait()

        at, kept = block_rows(index)
        mine[kept, :] = jnp.dot(
            emb[0, at, :], panel_t[0], preferred_element_type=jnp.float32
        ) + jnp.dot(emb[1, at, :], panel_t[1], preferred_element_type=jnp.float32)

    def weigh(index):
        at, kept = block_rows(index)
        total = mine[kept, :] + from_left[kept, :] + from_right[kept, :]
        weights_ref[at, :] = jnp.dot(
            total, system[...], precision=HIGH, preferred_element_type=jnp.float32
        )

    gram_at = pl.ds(0, half)

    def pass_right(index, at):
        @pl.when(has_left)
        def _():
            right_copy(index, at).wait_recv()

        @pl.when(has_right)
        def _():
            to_right[at, :] = mine[at, :] + from_left[at, :]
            right_copy(index, at).start()

    def pass_left(index, at):
        @pl.when(has_right)
        def _():
            left_copy(index, at).wait_recv()

        @pl.when(has_left)
        def _():
            to_left[at, :] = mine[at, :] + from_right[at, :]
            left_copy(index, at).start()

    def turn(index, _):
        left_index = index - col * LAG
        right_index = index - (cols_n - 1 - col) * LAG

        @pl.when(left_index == 0)
        def _():
            pass_right(left_index, gram_at)

        @pl.when((left_index >= 1) & (left_index < parts))
        def _():
            pass_right(left_index, part(left_index))

        @pl.when(right_index == 0)
        def _():
            pass_left(right_index, gram_at)

        @pl.when((right_index >= 1) & (right_index < parts))
        def _():
            pass_left(right_index, part(right_index))

        @pl.when((index % BLOCK_PARTS == 0) & (index < chunks))
        def _():
            multiply(index // BLOCK_PARTS)

        @pl.when(index == 2)
        def _():
            for side in range(2):
                padded = padded_panel(side).astype(jnp.bfloat16)
                for piece in range(3):
                    panels_ref[side, pl.ds(piece * 2 * rank, 2 * rank), :] = padded

        @pl.when(index == hops)
        def _():
            at = pl.ds(0, half)
            packed = mine[at, :] + from_left[at, :] + from_right[at, :]
            inside = lanes[0:half] < rank
            system[0:half, :] = jnp.where(inside, packed, 0.0)
            system[half:rank, :] = jnp.where(inside, pltpu.roll(packed, rank, 1), 0.0)

        @pl.when((index >= solve_from) & (index < weigh_from))
        def _():
            lax.fori_loop(
                (index - solve_from) * SOLVE_STEPS,
                (index - solve_from + 1) * SOLVE_STEPS,
                eliminate,
                0,
            )

        @pl.when(index == weigh_from)
        def _():
            system[rank : 2 * rank, :] = pltpu.roll(system[0:rank, :], rank, 1)

        since = index - (turns + 1 - 2 * blocks)

        @pl.when((since >= 0) & (since % 2 == 0))
        def _():
            weigh(since // 2)

        return 0

    lax.fori_loop(0, turns, turn, 0)

    for step in range(1, rows_n):
        row_copy(step).wait_send()

    def wait_sent(index, at):
        @pl.when(has_right)
        def _():
            right_copy(index, at).wait_send()

        @pl.when(has_left)
        def _():
            left_copy(index, at).wait_send()

    def sent(index, _):
        wait_sent(index, part(index))
        return 0

    wait_sent(0, gram_at)
    lax.fori_loop(1, parts, sent, 0)


def all_weights(emb3, own, rows_n, cols_n, rank):
    _, pairs, width = emb3.shape
    size = pairs // CHUNKS
    buffer = pltpu.VMEM((pairs + size, 2 * rank), jnp.float32)
    dma = pltpu.SemaphoreType.DMA
    return pl.pallas_call(
        functools.partial(weights_kernel, rows_n, cols_n, CHUNKS),
        out_shape=(
            jax.ShapeDtypeStruct(emb3.shape, emb3.dtype),
            jax.ShapeDtypeStruct((pairs, 2 * rank), jnp.float32),
            jax.ShapeDtypeStruct((2, 6 * rank, width), jnp.bfloat16),
        ),
        in_specs=[pl.BlockSpec(memory_space=pl.ANY), pl.BlockSpec(memory_space=pltpu.VMEM)],
        out_specs=(pl.BlockSpec(memory_space=pltpu.VMEM),) * 3,
        scratch_shapes=[
            pltpu.VMEM((rows_n,) + own.shape, jnp.float32),
            pltpu.VMEM((2, width, 2 * rank), jnp.bfloat16),
            pltpu.VMEM((2 * rank, 2 * rank), jnp.float32),
            buffer, buffer, buffer, buffer, buffer,
            dma, dma((rows_n,)), dma((rows_n,)),
            dma((CHUNKS + 1,)), dma((CHUNKS + 1,)), dma((CHUNKS + 1,)), dma((CHUNKS + 1,)),
        ],
        compiler_params=pltpu.CompilerParams(
            collective_id=0, has_side_effects=True, vmem_limit_bytes=40 * MIB
        ),
        cost_estimate=pl.CostEstimate(
            flops=8 * pairs * width * rank, bytes_accessed=2 * emb3.size, transcendentals=0
        ),
    )(emb3, own)


def subtract_kernel(emb_ref, weights_ref, panels_ref, out_ref):
    weights = weights_ref[...]
    first = weights.astype(jnp.bfloat16)
    rest = weights - first.astype(jnp.float32)
    second = rest.astype(jnp.bfloat16)
    third = (rest - second.astype(jnp.float32)).astype(jnp.bfloat16)
    pieces = jnp.concatenate([first, second, third], axis=1)
    for side in range(2):
        out_ref[side] = emb_ref[side].astype(jnp.float32) - jnp.dot(
            pieces, panels_ref[side], preferred_element_type=jnp.float32
        )


def subtract(emb3, weights, panels):
    _, pairs, width = emb3.shape
    block = min(256, pairs)
    return pl.pallas_call(
        subtract_kernel,
        grid=(pairs // block,),
        out_shape=jax.ShapeDtypeStruct(emb3.shape, jnp.float32),
        in_specs=[
            pl.BlockSpec((2, block, width), lambda i: (0, i, 0)),
            pl.BlockSpec((block, weights.shape[1]), lambda i: (i, 0)),
            pl.BlockSpec(panels.shape, lambda i: (0, 0, 0)),
        ],
        out_specs=pl.BlockSpec((2, block, width), lambda i: (0, i, 0)),
        compiler_params=pltpu.CompilerParams(vmem_limit_bytes=16 * MIB),
    )(emb3, weights, panels)


def per_device(rows_n, cols_n, embeddings, pick_rows):
    row_count, width = embeddings.shape
    rank = pick_rows.shape[0] * pick_rows.shape[1]
    own = own_picks(embeddings, pick_rows, rank // rows_n)
    emb3 = embeddings.reshape(2, row_count // 2, width)
    held, weights, panels = all_weights(emb3, own, rows_n, cols_n, rank)
    return subtract(held, weights, panels).reshape(row_count, width)


def solution(mesh):
    in_specs = (P("rows", "cols"), P())
    out_specs = P("rows", "cols")
    return jax.shard_map(
        functools.partial(per_device, mesh.shape["rows"], mesh.shape["cols"]),
        mesh=mesh, in_specs=in_specs, out_specs=out_specs, check_vma=False,
    )
```

```python
import functools

import jax
import jax.numpy as jnp
from jax import lax
from jax.experimental import pallas as pl
from jax.experimental.pallas import tpu as pltpu
from jax.sharding import PartitionSpec as P

HIGH = lax.Precision.HIGHEST
MESH = pl.DeviceIdType.MESH
GROUP = 16
CHUNKS = 32
LAG = 4
BLOCK_PARTS = 4
EARLY_BLOCKS = 6
SOLVE_STEPS = 4
MIB = 1024 * 1024


def own_picks_kernel(own_count, picks_ref, emb_ref, out_ref, groups, offsets, sems):
    row_count = emb_ref.shape[0]
    rounds, per_round = picks_ref.shape
    first = lax.axis_index("rows") * row_count

    def look(index, found):
        local = picks_ref[index // per_round, index % per_round] - first
        owned = (local >= 0) & (local < row_count) & (found < own_count)

        @pl.when(owned)
        def _():
            start = pl.multiple_of((local // GROUP) * GROUP, GROUP)
            offsets[found] = local - start
            pltpu.make_async_copy(
                emb_ref.at[pl.ds(start, GROUP), :], groups.at[found], sems.at[found]
            ).start()

        return found + owned.astype(jnp.int32)

    lax.fori_loop(0, rounds * per_round, look, jnp.int32(0), unroll=8)
    for slot in range(own_count):
        pltpu.make_async_copy(
            emb_ref.at[pl.ds(0, GROUP), :], groups.at[slot], sems.at[slot]
        ).wait()
        rows = groups[slot].astype(jnp.float32)
        inside = lax.broadcasted_iota(jnp.int32, rows.shape, 0) == offsets[slot]
        out_ref[pl.ds(slot, 1), :] = jnp.sum(jnp.where(inside, rows, 0.0), axis=0, keepdims=True)


def own_picks(embeddings, picks, own_count):
    width = embeddings.shape[1]
    return pl.pallas_call(
        functools.partial(own_picks_kernel, own_count),
        out_shape=jax.ShapeDtypeStruct((own_count, width), jnp.float32),
        in_specs=[
            pl.BlockSpec(memory_space=pltpu.SMEM),
            pl.BlockSpec(memory_space=pl.ANY),
        ],
        out_specs=pl.BlockSpec(memory_space=pltpu.VMEM),
        scratch_shapes=[
            pltpu.VMEM((own_count, GROUP, width), embeddings.dtype),
            pltpu.SMEM((own_count,), jnp.int32),
            pltpu.SemaphoreType.DMA((own_count,)),
        ],
        compiler_params=pltpu.CompilerParams(vmem_limit_bytes=52 * MIB),
    )(picks, embeddings)


def residual_rows(emb, weights, panel):
    first = weights.astype(jnp.bfloat16)
    rest = weights - first.astype(jnp.float32)
    second = rest.astype(jnp.bfloat16)
    third = (rest - second.astype(jnp.float32)).astype(jnp.bfloat16)
    pieces = jnp.concatenate([first, second, third], axis=1)
    return emb.astype(jnp.float32) - jnp.dot(pieces, panel, preferred_element_type=jnp.float32)


def weights_kernel(
    rows_n, cols_n, chunks, emb, own_ref, weights_ref, panels_ref, early_ref,
    gathered, panel_t, system, mine, from_left, from_right, to_right, to_left,
    row_send, row_recv, right_send, left_recv, left_send, right_recv,
):
    own_count, width = own_ref.shape
    rank = rows_n * own_count
    half = rank // 2
    size = weights_ref.shape[0] // chunks
    row = lax.axis_index("rows")
    col = lax.axis_index("cols")
    has_left = col > 0
    has_right = col < cols_n - 1

    barrier = pltpu.get_barrier_semaphore()
    for step in range(1, rows_n):
        pl.semaphore_signal(
            barrier, inc=1, device_id={"rows": lax.rem(row + step, rows_n)}, device_id_type=MESH
        )

    @pl.when(has_left)
    def _():
        pl.semaphore_signal(barrier, inc=1, device_id={"cols": col - 1}, device_id_type=MESH)

    @pl.when(has_right)
    def _():
        pl.semaphore_signal(barrier, inc=1, device_id={"cols": col + 1}, device_id_type=MESH)

    @pl.when(jnp.logical_not(has_left))
    def _():
        from_left[...] = jnp.zeros_like(from_left)

    @pl.when(jnp.logical_not(has_right))
    def _():
        from_right[...] = jnp.zeros_like(from_right)

    pl.semaphore_wait(
        barrier, rows_n - 1 + has_left.astype(jnp.int32) + has_right.astype(jnp.int32)
    )

    def row_copy(step):
        return pltpu.make_async_remote_copy(
            src_ref=own_ref,
            dst_ref=gathered.at[row],
            send_sem=row_send.at[step],
            recv_sem=row_recv.at[row],
            device_id={"rows": lax.rem(row + step, rows_n)},
            device_id_type=MESH,
        )

    for step in range(1, rows_n):
        row_copy(step).start()
    gathered[row] = own_ref[...]
    for step in range(1, rows_n):
        source = lax.rem(row + step, rows_n)
        pltpu.make_async_remote_copy(
            src_ref=own_ref,
            dst_ref=gathered.at[source],
            send_sem=row_send.at[step],
            recv_sem=row_recv.at[source],
            device_id={"rows": source},
            device_id_type=MESH,
        ).wait_recv()

    def padded_panel(side):
        panel = jnp.concatenate([gathered[owner] for owner in range(rows_n)], axis=0)
        nothing = jnp.zeros_like(panel)
        return jnp.concatenate([panel, nothing] if side == 0 else [nothing, panel], axis=0)

    for side in range(2):
        panel_t[side] = padded_panel(side).T.astype(jnp.bfloat16)
    panel16 = padded_panel(0)[:rank].astype(jnp.bfloat16)

    mine[pl.ds(0, half), :] = jnp.dot(
        panel16[:half], panel_t[0], preferred_element_type=jnp.float32
    ) + jnp.dot(panel16[half:], panel_t[1], preferred_element_type=jnp.float32)

    def part(index):
        return pl.ds(pl.multiple_of(index * size, size), size)

    def right_copy(index, at):
        return pltpu.make_async_remote_copy(
            src_ref=to_right.at[at],
            dst_ref=from_left.at[at],
            send_sem=right_send.at[index],
            recv_sem=left_recv.at[index],
            device_id={"cols": lax.rem(col + 1, cols_n)},
            device_id_type=MESH,
        )

    def left_copy(index, at):
        return pltpu.make_async_remote_copy(
            src_ref=to_left.at[at],
            dst_ref=from_right.at[at],
            send_sem=left_send.at[index],
            recv_sem=right_recv.at[index],
            device_id={"cols": lax.rem(col + cols_n - 1, cols_n)},
            device_id_type=MESH,
        )

    parts = chunks + 1
    hops = (cols_n - 1) * LAG
    solve_from = hops + 1
    solve_turns = rank // SOLVE_STEPS
    weigh_from = solve_from + solve_turns
    turns = parts + hops
    assert turns + 1 - 2 * (chunks // BLOCK_PARTS) >= weigh_from
    lanes = lax.broadcasted_iota(jnp.int32, (rank, 2 * rank), 1)
    sublanes = lax.broadcasted_iota(jnp.int32, (rank, 2 * rank), 0)

    def eliminate(step, _):
        now = system[0:rank, :]
        picked = system[pl.ds(step, 1), :]
        on_lane = lanes == step
        on_row = sublanes == step
        column = jnp.sum(jnp.where(on_lane, now, 0.0), axis=1, keepdims=True)
        pivot = jnp.sum(jnp.where(on_lane[0:1], picked, 0.0), axis=1, keepdims=True)
        new_row = jnp.where(on_lane[0:1], 1.0, picked) / pivot
        rest = jnp.where(on_lane, 0.0, now) - column * new_row
        system[0:rank, :] = jnp.where(on_row, jnp.broadcast_to(new_row, now.shape), rest)
        return 0

    block = BLOCK_PARTS * size
    blocks = chunks // BLOCK_PARTS

    def block_rows(index):
        start = pl.multiple_of(index * block, block)
        return pl.ds(start, block), pl.ds(pl.multiple_of(start + size, size), block)

    def multiply(index):
        at, kept = block_rows(index)
        mine[kept, :] = jnp.dot(
            emb[0, at, :], panel_t[0], preferred_element_type=jnp.float32
        ) + jnp.dot(emb[1, at, :], panel_t[1], preferred_element_type=jnp.float32)

    def weigh(index):
        at, kept = block_rows(index)
        total = mine[kept, :] + from_left[kept, :] + from_right[kept, :]
        weights_ref[at, :] = jnp.dot(
            total, system[...], precision=HIGH, preferred_element_type=jnp.float32
        )

    gram_at = pl.ds(0, half)

    def pass_right(index, at):
        @pl.when(has_left)
        def _():
            right_copy(index, at).wait_recv()

        @pl.when(has_right)
        def _():
            to_right[at, :] = mine[at, :] + from_left[at, :]
            right_copy(index, at).start()

    def pass_left(index, at):
        @pl.when(has_right)
        def _():
            left_copy(index, at).wait_recv()

        @pl.when(has_left)
        def _():
            to_left[at, :] = mine[at, :] + from_right[at, :]
            left_copy(index, at).start()

    def turn(index, _):
        left_index = index - col * LAG
        right_index = index - (cols_n - 1 - col) * LAG

        @pl.when(left_index == 0)
        def _():
            pass_right(left_index, gram_at)

        @pl.when((left_index >= 1) & (left_index < parts))
        def _():
            pass_right(left_index, part(left_index))

        @pl.when(right_index == 0)
        def _():
            pass_left(right_index, gram_at)

        @pl.when((right_index >= 1) & (right_index < parts))
        def _():
            pass_left(right_index, part(right_index))

        @pl.when((index % BLOCK_PARTS == 0) & (index < chunks))
        def _():
            multiply(index // BLOCK_PARTS)

        @pl.when(index == 2)
        def _():
            for side in range(2):
                padded = padded_panel(side).astype(jnp.bfloat16)
                for piece in range(3):
                    panels_ref[side, pl.ds(piece * 2 * rank, 2 * rank), :] = padded

        @pl.when(index == hops)
        def _():
            at = pl.ds(0, half)
            packed = mine[at, :] + from_left[at, :] + from_right[at, :]
            inside = lanes[0:half] < rank
            system[0:half, :] = jnp.where(inside, packed, 0.0)
            system[half:rank, :] = jnp.where(inside, pltpu.roll(packed, rank, 1), 0.0)

        @pl.when((index >= solve_from) & (index < weigh_from))
        def _():
            lax.fori_loop(
                (index - solve_from) * SOLVE_STEPS,
                (index - solve_from + 1) * SOLVE_STEPS,
                eliminate,
                0,
            )

        @pl.when(index == weigh_from)
        def _():
            system[rank : 2 * rank, :] = pltpu.roll(system[0:rank, :], rank, 1)

        since = index - (turns + 1 - 2 * blocks)

        @pl.when((since >= 0) & (since % 2 == 1) & (since < 2 * EARLY_BLOCKS))
        def _():
            at, _ = block_rows(since // 2)
            for side in range(2):
                early_ref[side, at, :] = residual_rows(
                    emb[side, at, :], weights_ref[at, :], panels_ref[side]
                )

        @pl.when((since >= 0) & (since % 2 == 0))
        def _():
            weigh(since // 2)

        return 0

    lax.fori_loop(0, turns, turn, 0)

    for step in range(1, rows_n):
        row_copy(step).wait_send()

    def wait_sent(index, at):
        @pl.when(has_right)
        def _():
            right_copy(index, at).wait_send()

        @pl.when(has_left)
        def _():
            left_copy(index, at).wait_send()

    def sent(index, _):
        wait_sent(index, part(index))
        return 0

    wait_sent(0, gram_at)
    lax.fori_loop(1, parts, sent, 0)


def all_weights(emb3, own, rows_n, cols_n, rank):
    _, pairs, width = emb3.shape
    size = pairs // CHUNKS
    buffer = pltpu.VMEM((pairs + size, 2 * rank), jnp.float32)
    dma = pltpu.SemaphoreType.DMA
    return pl.pallas_call(
        functools.partial(weights_kernel, rows_n, cols_n, CHUNKS),
        out_shape=(
            jax.ShapeDtypeStruct((pairs, 2 * rank), jnp.float32),
            jax.ShapeDtypeStruct((2, 6 * rank, width), jnp.bfloat16),
            jax.ShapeDtypeStruct((2, EARLY_BLOCKS * BLOCK_PARTS * size, width), jnp.float32),
        ),
        in_specs=[pl.BlockSpec(memory_space=pltpu.VMEM)] * 2,
        out_specs=(pl.BlockSpec(memory_space=pltpu.VMEM),) * 3,
        scratch_shapes=[
            pltpu.VMEM((rows_n,) + own.shape, jnp.float32),
            pltpu.VMEM((2, width, 2 * rank), jnp.bfloat16),
            pltpu.VMEM((2 * rank, 2 * rank), jnp.float32),
            buffer, buffer, buffer, buffer, buffer,
            dma((rows_n,)), dma((rows_n,)),
            dma((CHUNKS + 1,)), dma((CHUNKS + 1,)), dma((CHUNKS + 1,)), dma((CHUNKS + 1,)),
        ],
        compiler_params=pltpu.CompilerParams(
            collective_id=0, has_side_effects=True, vmem_limit_bytes=24 * MIB
        ),
        cost_estimate=pl.CostEstimate(
            flops=8 * pairs * width * rank, bytes_accessed=2 * emb3.size, transcendentals=0
        ),
    )(emb3, own)


def last_kernel(
    block, emb_ref, weights_ref, panels_ref, early_ref, out_ref,
    emb, late, emb_sem, early_sems, late_sems,
):
    early = early_ref.shape[1] // block
    late_count = late.shape[1] // block
    load = pltpu.make_async_copy(emb_ref.at[:, pl.ds(early * block, late_count * block), :], emb, emb_sem)
    load.start()
    copies = []
    for index in range(early):
        at = pl.ds(index * block, block)
        for side in range(2):
            copies.append(
                pltpu.make_async_copy(
                    early_ref.at[side, at], out_ref.at[side, at], early_sems.at[index, side]
                )
            )
            copies[-1].start()
    load.wait()
    for index in range(late_count):
        here = pl.ds(index * block, block)
        at = pl.ds((early + index) * block, block)
        for side in range(2):
            late[side, here, :] = residual_rows(
                emb[side, here, :], weights_ref[at, :], panels_ref[side]
            )
            copies.append(
                pltpu.make_async_copy(
                    late.at[side, here], out_ref.at[side, at], late_sems.at[index, side]
                )
            )
            copies[-1].start()
    for copy in copies:
        copy.wait()


def last_rows(emb3, weights, panels, early):
    _, pairs, width = emb3.shape
    block = BLOCK_PARTS * (pairs // CHUNKS)
    late = pairs - early.shape[1]
    dma = pltpu.SemaphoreType.DMA
    anywhere = pl.BlockSpec(memory_space=pl.ANY)
    inside = pl.BlockSpec(memory_space=pltpu.VMEM)
    return pl.pallas_call(
        functools.partial(last_kernel, block),
        out_shape=jax.ShapeDtypeStruct(emb3.shape, jnp.float32),
        in_specs=[anywhere, inside, inside, anywhere],
        out_specs=anywhere,
        scratch_shapes=[
            pltpu.VMEM((2, late, width), emb3.dtype),
            pltpu.VMEM((2, late, width), jnp.float32),
            dma, dma((early.shape[1] // block, 2)), dma((late // block, 2)),
        ],
        compiler_params=pltpu.CompilerParams(vmem_limit_bytes=24 * MIB),
    )(emb3, weights, panels, early)


def per_device(rows_n, cols_n, embeddings, pick_rows):
    row_count, width = embeddings.shape
    rank = pick_rows.shape[0] * pick_rows.shape[1]
    own = own_picks(embeddings, pick_rows, rank // rows_n)
    emb3 = embeddings.reshape(2, row_count // 2, width)
    parts = all_weights(emb3, own, rows_n, cols_n, rank)
    return last_rows(emb3, *parts).reshape(row_count, width)


def solution(mesh):
    in_specs = (P("rows", "cols"), P())
    out_specs = P("rows", "cols")
    return jax.shard_map(
        functools.partial(per_device, mesh.shape["rows"], mesh.shape["cols"]),
        mesh=mesh, in_specs=in_specs, out_specs=out_specs, check_vma=False,
    )
```

```python
import functools

import jax
import jax.numpy as jnp
from jax import lax
from jax.experimental import pallas as pl
from jax.experimental.pallas import tpu as pltpu
from jax.sharding import PartitionSpec as P

HIGH = lax.Precision.HIGHEST
MESH = pl.DeviceIdType.MESH
GROUP = 16
CHUNKS = 64
LAG = 8
BLOCK_PARTS = 8
STRIDE = 4
EARLY_BLOCKS = 6
SOLVE_STEPS = 2
MIB = 1024 * 1024


def own_picks_kernel(own_count, picks_ref, emb_ref, out_ref, groups, offsets, sems):
    row_count = emb_ref.shape[0]
    rounds, per_round = picks_ref.shape
    first = lax.axis_index("rows") * row_count

    def look(index, found):
        local = picks_ref[index // per_round, index % per_round] - first
        owned = (local >= 0) & (local < row_count) & (found < own_count)

        @pl.when(owned)
        def _():
            start = pl.multiple_of((local // GROUP) * GROUP, GROUP)
            offsets[found] = local - start
            pltpu.make_async_copy(
                emb_ref.at[pl.ds(start, GROUP), :], groups.at[found], sems.at[found]
            ).start()

        return found + owned.astype(jnp.int32)

    lax.fori_loop(0, rounds * per_round, look, jnp.int32(0), unroll=8)
    for slot in range(own_count):
        pltpu.make_async_copy(
            emb_ref.at[pl.ds(0, GROUP), :], groups.at[slot], sems.at[slot]
        ).wait()
        rows = groups[slot].astype(jnp.float32)
        inside = lax.broadcasted_iota(jnp.int32, rows.shape, 0) == offsets[slot]
        out_ref[pl.ds(slot, 1), :] = jnp.sum(jnp.where(inside, rows, 0.0), axis=0, keepdims=True)


def own_picks(embeddings, picks, own_count):
    width = embeddings.shape[1]
    return pl.pallas_call(
        functools.partial(own_picks_kernel, own_count),
        out_shape=jax.ShapeDtypeStruct((own_count, width), jnp.float32),
        in_specs=[
            pl.BlockSpec(memory_space=pltpu.SMEM),
            pl.BlockSpec(memory_space=pl.ANY),
        ],
        out_specs=pl.BlockSpec(memory_space=pltpu.VMEM),
        scratch_shapes=[
            pltpu.VMEM((own_count, GROUP, width), embeddings.dtype),
            pltpu.SMEM((own_count,), jnp.int32),
            pltpu.SemaphoreType.DMA((own_count,)),
        ],
        compiler_params=pltpu.CompilerParams(vmem_limit_bytes=52 * MIB),
    )(picks, embeddings)


def residual_rows(emb, weights, panel):
    first = weights.astype(jnp.bfloat16)
    rest = weights - first.astype(jnp.float32)
    second = rest.astype(jnp.bfloat16)
    third = (rest - second.astype(jnp.float32)).astype(jnp.bfloat16)
    pieces = jnp.concatenate([first, second, third], axis=1)
    return emb.astype(jnp.float32) - jnp.dot(pieces, panel, preferred_element_type=jnp.float32)


def weights_kernel(
    rows_n, cols_n, chunks, emb, own_ref, weights_ref, panels_ref, early_ref, system,
    gathered, panel_t, mine, from_left, from_right, to_right, to_left,
    row_send, row_recv, right_send, left_recv, left_send, right_recv,
):
    own_count, width = own_ref.shape
    rank = rows_n * own_count
    half = rank // 2
    size = weights_ref.shape[0] // chunks
    row = lax.axis_index("rows")
    col = lax.axis_index("cols")
    has_left = col > 0
    has_right = col < cols_n - 1

    barrier = pltpu.get_barrier_semaphore()
    for step in range(1, rows_n):
        pl.semaphore_signal(
            barrier, inc=1, device_id={"rows": lax.rem(row + step, rows_n)}, device_id_type=MESH
        )

    @pl.when(has_left)
    def _():
        pl.semaphore_signal(barrier, inc=1, device_id={"cols": col - 1}, device_id_type=MESH)

    @pl.when(has_right)
    def _():
        pl.semaphore_signal(barrier, inc=1, device_id={"cols": col + 1}, device_id_type=MESH)

    @pl.when(jnp.logical_not(has_left))
    def _():
        from_left[...] = jnp.zeros_like(from_left)

    @pl.when(jnp.logical_not(has_right))
    def _():
        from_right[...] = jnp.zeros_like(from_right)

    pl.semaphore_wait(
        barrier, rows_n - 1 + has_left.astype(jnp.int32) + has_right.astype(jnp.int32)
    )

    def row_copy(step):
        return pltpu.make_async_remote_copy(
            src_ref=own_ref,
            dst_ref=gathered.at[row],
            send_sem=row_send.at[step],
            recv_sem=row_recv.at[row],
            device_id={"rows": lax.rem(row + step, rows_n)},
            device_id_type=MESH,
        )

    for step in range(1, rows_n):
        row_copy(step).start()
    gathered[row] = own_ref[...]
    for step in range(1, rows_n):
        source = lax.rem(row + step, rows_n)
        pltpu.make_async_remote_copy(
            src_ref=own_ref,
            dst_ref=gathered.at[source],
            send_sem=row_send.at[step],
            recv_sem=row_recv.at[source],
            device_id={"rows": source},
            device_id_type=MESH,
        ).wait_recv()

    def padded_panel(side):
        panel = jnp.concatenate([gathered[owner] for owner in range(rows_n)], axis=0)
        nothing = jnp.zeros_like(panel)
        return jnp.concatenate([panel, nothing] if side == 0 else [nothing, panel], axis=0)

    for side in range(2):
        panel_t[side] = padded_panel(side).T.astype(jnp.bfloat16)
    panel16 = padded_panel(0)[:rank].astype(jnp.bfloat16)

    mine[pl.ds(0, half), :] = jnp.dot(
        panel16[:half], panel_t[0], preferred_element_type=jnp.float32
    ) + jnp.dot(panel16[half:], panel_t[1], preferred_element_type=jnp.float32)

    def part(index):
        return pl.ds(pl.multiple_of(index * size, size), size)

    def right_copy(index, at):
        return pltpu.make_async_remote_copy(
            src_ref=to_right.at[at],
            dst_ref=from_left.at[at],
            send_sem=right_send,
            recv_sem=left_recv.at[index],
            device_id={"cols": lax.rem(col + 1, cols_n)},
            device_id_type=MESH,
        )

    def left_copy(index, at):
        return pltpu.make_async_remote_copy(
            src_ref=to_left.at[at],
            dst_ref=from_right.at[at],
            send_sem=left_send,
            recv_sem=right_recv.at[index],
            device_id={"cols": lax.rem(col + cols_n - 1, cols_n)},
            device_id_type=MESH,
        )

    parts = chunks + 1
    hops = (cols_n - 1) * LAG
    solve_from = hops + 1
    solve_turns = rank // SOLVE_STEPS
    weigh_from = solve_from + solve_turns
    turns = parts + hops
    assert turns - 1 - STRIDE * (chunks // BLOCK_PARTS - 1) >= weigh_from
    lanes = lax.broadcasted_iota(jnp.int32, (rank, 2 * rank), 1)
    sublanes = lax.broadcasted_iota(jnp.int32, (rank, 2 * rank), 0)

    def eliminate(step, _):
        now = system[0:rank, :]
        picked = system[pl.ds(step, 1), :]
        on_lane = lanes == step
        on_row = sublanes == step
        column = jnp.sum(jnp.where(on_lane, now, 0.0), axis=1, keepdims=True)
        pivot = jnp.sum(jnp.where(on_lane[0:1], picked, 0.0), axis=1, keepdims=True)
        new_row = jnp.where(on_lane[0:1], 1.0, picked) / pivot
        rest = jnp.where(on_lane, 0.0, now) - column * new_row
        system[0:rank, :] = jnp.where(on_row, jnp.broadcast_to(new_row, now.shape), rest)
        return 0

    block = BLOCK_PARTS * size
    blocks = chunks // BLOCK_PARTS

    def block_rows(index):
        start = pl.multiple_of(index * block, block)
        return pl.ds(start, block), pl.ds(pl.multiple_of(start + size, size), block)

    def multiply(index):
        at, kept = block_rows(index)
        mine[kept, :] = jnp.dot(
            emb[0, at, :], panel_t[0], preferred_element_type=jnp.float32
        ) + jnp.dot(emb[1, at, :], panel_t[1], preferred_element_type=jnp.float32)

    def block_sum(kept):
        return mine[kept, :] + from_left[kept, :] + from_right[kept, :]

    def weigh(index):
        at, kept = block_rows(index)
        weights_ref[at, :] = jnp.dot(
            block_sum(kept), system[...], precision=HIGH, preferred_element_type=jnp.float32
        )

    gram_at = pl.ds(0, half)

    def pass_right(index, at):
        @pl.when(has_left)
        def _():
            right_copy(index, at).wait_recv()

        @pl.when(has_right)
        def _():
            to_right[at, :] = mine[at, :] + from_left[at, :]
            right_copy(index, at).start()

    def pass_left(index, at):
        @pl.when(has_right)
        def _():
            left_copy(index, at).wait_recv()

        @pl.when(has_left)
        def _():
            to_left[at, :] = mine[at, :] + from_right[at, :]
            left_copy(index, at).start()

    def turn(index, _):
        left_index = index - col * LAG
        right_index = index - (cols_n - 1 - col) * LAG

        @pl.when(left_index == 0)
        def _():
            pass_right(left_index, gram_at)

        @pl.when((left_index >= 1) & (left_index < parts))
        def _():
            pass_right(left_index, part(left_index))

        @pl.when(right_index == 0)
        def _():
            pass_left(right_index, gram_at)

        @pl.when((right_index >= 1) & (right_index < parts))
        def _():
            pass_left(right_index, part(right_index))

        @pl.when((index % BLOCK_PARTS == 0) & (index < chunks))
        def _():
            multiply(index // BLOCK_PARTS)

        @pl.when(index == 2)
        def _():
            for side in range(2):
                padded = padded_panel(side).astype(jnp.bfloat16)
                for piece in range(3):
                    panels_ref[side, pl.ds(piece * 2 * rank, 2 * rank), :] = padded

        @pl.when(index == hops)
        def _():
            at = pl.ds(0, half)
            packed = mine[at, :] + from_left[at, :] + from_right[at, :]
            inside = lanes[0:half] < rank
            system[0:half, :] = jnp.where(inside, packed, 0.0)
            system[half:rank, :] = jnp.where(inside, pltpu.roll(packed, rank, 1), 0.0)

        @pl.when((index >= solve_from) & (index < weigh_from))
        def _():
            lax.fori_loop(
                (index - solve_from) * SOLVE_STEPS,
                (index - solve_from + 1) * SOLVE_STEPS,
                eliminate,
                0,
            )

        @pl.when(index == weigh_from)
        def _():
            system[rank : 2 * rank, :] = pltpu.roll(system[0:rank, :], rank, 1)

        since = index - (turns - 1 - STRIDE * (blocks - 1))

        @pl.when((since >= 0) & (since % STRIDE == STRIDE // 2) & (since < STRIDE * EARLY_BLOCKS))
        def _():
            at, _ = block_rows(since // STRIDE)
            for side in range(2):
                early_ref[side, at, :] = residual_rows(
                    emb[side, at, :], weights_ref[at, :], panels_ref[side]
                )

        @pl.when((since >= 0) & (since % STRIDE == 0) & (since < STRIDE * (blocks - 1)))
        def _():
            weigh(since // STRIDE)

        return 0

    lax.fori_loop(0, turns, turn, 0)
    at, kept = block_rows(blocks - 1)
    weights_ref[at, :] = block_sum(kept)

    for step in range(1, rows_n):
        row_copy(step).wait_send()

    def wait_sent(index, at):
        @pl.when(has_right)
        def _():
            right_copy(index, at).wait_send()

        @pl.when(has_left)
        def _():
            left_copy(index, at).wait_send()

    wait_sent(0, pl.ds(size - half, chunks * size + half))


def all_weights(emb3, own, rows_n, cols_n, rank):
    _, pairs, width = emb3.shape
    size = pairs // CHUNKS
    buffer = pltpu.VMEM((pairs + size, 2 * rank), jnp.float32)
    dma = pltpu.SemaphoreType.DMA
    return pl.pallas_call(
        functools.partial(weights_kernel, rows_n, cols_n, CHUNKS),
        out_shape=(
            jax.ShapeDtypeStruct((pairs, 2 * rank), jnp.float32),
            jax.ShapeDtypeStruct((2, 6 * rank, width), jnp.bfloat16),
            jax.ShapeDtypeStruct((2, EARLY_BLOCKS * BLOCK_PARTS * size, width), jnp.float32),
            jax.ShapeDtypeStruct((2 * rank, 2 * rank), jnp.float32),
        ),
        in_specs=[pl.BlockSpec(memory_space=pltpu.VMEM)] * 2,
        out_specs=(pl.BlockSpec(memory_space=pltpu.VMEM),) * 4,
        scratch_shapes=[
            pltpu.VMEM((rows_n,) + own.shape, jnp.float32),
            pltpu.VMEM((2, width, 2 * rank), jnp.bfloat16),
            buffer, buffer, buffer, buffer, buffer,
            dma((rows_n,)), dma((rows_n,)),
            dma, dma((CHUNKS + 1,)), dma, dma((CHUNKS + 1,)),
        ],
        compiler_params=pltpu.CompilerParams(
            collective_id=0, has_side_effects=True, vmem_limit_bytes=16 * MIB
        ),
        cost_estimate=pl.CostEstimate(
            flops=8 * pairs * width * rank, bytes_accessed=2 * emb3.size, transcendentals=0
        ),
    )(emb3, own)


def last_kernel(
    block, emb_ref, weights_ref, panels_ref, early_ref, system_ref, out_ref,
    emb, late, emb_sem, early_sems, late_sems,
):
    early = early_ref.shape[1] // block
    late_count = late.shape[1] // block
    load = pltpu.make_async_copy(emb_ref.at[:, pl.ds(early * block, late_count * block), :], emb, emb_sem)
    load.start()
    copies = []
    for index in range(early):
        at = pl.ds(index * block, block)
        for side in range(2):
            copies.append(
                pltpu.make_async_copy(
                    early_ref.at[side, at], out_ref.at[side, at], early_sems.at[index, side]
                )
            )
            copies[-1].start()
    load.wait()
    for index in range(late_count):
        here = pl.ds(index * block, block)
        at = pl.ds((early + index) * block, block)
        weights = weights_ref[at, :]
        if index == late_count - 1:
            weights = jnp.dot(
                weights, system_ref[...], precision=HIGH, preferred_element_type=jnp.float32
            )
        for side in range(2):
            late[side, here, :] = residual_rows(emb[side, here, :], weights, panels_ref[side])
            copies.append(
                pltpu.make_async_copy(
                    late.at[side, here], out_ref.at[side, at], late_sems.at[index, side]
                )
            )
            copies[-1].start()
    for copy in copies:
        copy.wait()


def last_rows(emb3, weights, panels, early, system):
    _, pairs, width = emb3.shape
    block = BLOCK_PARTS * (pairs // CHUNKS)
    late = pairs - early.shape[1]
    dma = pltpu.SemaphoreType.DMA
    anywhere = pl.BlockSpec(memory_space=pl.ANY)
    inside = pl.BlockSpec(memory_space=pltpu.VMEM)
    return pl.pallas_call(
        functools.partial(last_kernel, block),
        out_shape=jax.ShapeDtypeStruct(emb3.shape, jnp.float32),
        in_specs=[anywhere, inside, inside, anywhere, inside],
        out_specs=anywhere,
        scratch_shapes=[
            pltpu.VMEM((2, late, width), emb3.dtype),
            pltpu.VMEM((2, late, width), jnp.float32),
            dma, dma((early.shape[1] // block, 2)), dma((late // block, 2)),
        ],
        compiler_params=pltpu.CompilerParams(vmem_limit_bytes=12 * MIB),
    )(emb3, weights, panels, early, system)


def per_device(rows_n, cols_n, embeddings, pick_rows):
    row_count, width = embeddings.shape
    rank = pick_rows.shape[0] * pick_rows.shape[1]
    own = own_picks(embeddings, pick_rows, rank // rows_n)
    emb3 = embeddings.reshape(2, row_count // 2, width)
    parts = all_weights(emb3, own, rows_n, cols_n, rank)
    return last_rows(emb3, *parts).reshape(row_count, width)


def solution(mesh):
    in_specs = (P("rows", "cols"), P())
    out_specs = P("rows", "cols")
    return jax.shard_map(
        functools.partial(per_device, mesh.shape["rows"], mesh.shape["cols"]),
        mesh=mesh, in_specs=in_specs, out_specs=out_specs, check_vma=False,
    )
```

```python
import functools

import jax
import jax.numpy as jnp
from jax import lax
from jax.experimental import pallas as pl
from jax.experimental.pallas import tpu as pltpu
from jax.sharding import PartitionSpec as P

HIGH = lax.Precision.HIGHEST
MESH = pl.DeviceIdType.MESH
GROUP = 16
CHUNKS = 64
LAG = 6
BLOCK_PARTS = 8
STRIDE = 4
EARLY_BLOCKS = 5
LATE_WEIGHED = 2
SOLVE_STEPS = 2
MIB = 1024 * 1024


def own_picks_kernel(own_count, picks_ref, emb_ref, out_ref, groups, offsets, sems):
    row_count = emb_ref.shape[0]
    rounds, per_round = picks_ref.shape
    first = lax.axis_index("rows") * row_count

    def look(index, found):
        local = picks_ref[index // per_round, index % per_round] - first
        owned = (local >= 0) & (local < row_count) & (found < own_count)

        @pl.when(owned)
        def _():
            start = pl.multiple_of((local // GROUP) * GROUP, GROUP)
            offsets[found] = local - start
            pltpu.make_async_copy(
                emb_ref.at[pl.ds(start, GROUP), :], groups.at[found], sems.at[found]
            ).start()

        return found + owned.astype(jnp.int32)

    lax.fori_loop(0, rounds * per_round, look, jnp.int32(0), unroll=8)
    for slot in range(own_count):
        pltpu.make_async_copy(
            emb_ref.at[pl.ds(0, GROUP), :], groups.at[slot], sems.at[slot]
        ).wait()
        rows = groups[slot].astype(jnp.float32)
        inside = lax.broadcasted_iota(jnp.int32, rows.shape, 0) == offsets[slot]
        out_ref[pl.ds(slot, 1), :] = jnp.sum(jnp.where(inside, rows, 0.0), axis=0, keepdims=True)


def own_picks(embeddings, picks, own_count):
    width = embeddings.shape[1]
    return pl.pallas_call(
        functools.partial(own_picks_kernel, own_count),
        out_shape=jax.ShapeDtypeStruct((own_count, width), jnp.float32),
        in_specs=[
            pl.BlockSpec(memory_space=pltpu.SMEM),
            pl.BlockSpec(memory_space=pl.ANY),
        ],
        out_specs=pl.BlockSpec(memory_space=pltpu.VMEM),
        scratch_shapes=[
            pltpu.VMEM((own_count, GROUP, width), embeddings.dtype),
            pltpu.SMEM((own_count,), jnp.int32),
            pltpu.SemaphoreType.DMA((own_count,)),
        ],
        compiler_params=pltpu.CompilerParams(vmem_limit_bytes=52 * MIB),
    )(picks, embeddings)


def residual_rows(emb, weights, panel):
    first = weights.astype(jnp.bfloat16)
    rest = weights - first.astype(jnp.float32)
    second = rest.astype(jnp.bfloat16)
    third = (rest - second.astype(jnp.float32)).astype(jnp.bfloat16)
    pieces = jnp.concatenate([first, second, third], axis=1)
    return emb.astype(jnp.float32) - jnp.dot(pieces, panel, preferred_element_type=jnp.float32)


def weights_kernel(
    rows_n, cols_n, chunks, emb, own_ref, weights_ref, panels_ref, early_ref, system,
    gathered, panel_t, mine, from_left, from_right, to_right, to_left,
    row_send, row_recv, right_send, left_recv, left_send, right_recv,
):
    own_count, width = own_ref.shape
    rank = rows_n * own_count
    half = rank // 2
    size = weights_ref.shape[0] // chunks
    row = lax.axis_index("rows")
    col = lax.axis_index("cols")
    has_left = col > 0
    has_right = col < cols_n - 1

    barrier = pltpu.get_barrier_semaphore()
    for step in range(1, rows_n):
        pl.semaphore_signal(
            barrier, inc=1, device_id={"rows": lax.rem(row + step, rows_n)}, device_id_type=MESH
        )

    @pl.when(has_left)
    def _():
        pl.semaphore_signal(barrier, inc=1, device_id={"cols": col - 1}, device_id_type=MESH)

    @pl.when(has_right)
    def _():
        pl.semaphore_signal(barrier, inc=1, device_id={"cols": col + 1}, device_id_type=MESH)

    @pl.when(jnp.logical_not(has_left))
    def _():
        from_left[...] = jnp.zeros_like(from_left)

    @pl.when(jnp.logical_not(has_right))
    def _():
        from_right[...] = jnp.zeros_like(from_right)

    pl.semaphore_wait(
        barrier, rows_n - 1 + has_left.astype(jnp.int32) + has_right.astype(jnp.int32)
    )

    def row_copy(step):
        return pltpu.make_async_remote_copy(
            src_ref=own_ref,
            dst_ref=gathered.at[row],
            send_sem=row_send.at[step],
            recv_sem=row_recv.at[row],
            device_id={"rows": lax.rem(row + step, rows_n)},
            device_id_type=MESH,
        )

    for step in range(1, rows_n):
        row_copy(step).start()
    gathered[row] = own_ref[...]
    for step in range(1, rows_n):
        source = lax.rem(row + step, rows_n)
        pltpu.make_async_remote_copy(
            src_ref=own_ref,
            dst_ref=gathered.at[source],
            send_sem=row_send.at[step],
            recv_sem=row_recv.at[source],
            device_id={"rows": source},
            device_id_type=MESH,
        ).wait_recv()

    def padded_panel(side):
        panel = jnp.concatenate([gathered[owner] for owner in range(rows_n)], axis=0)
        nothing = jnp.zeros_like(panel)
        return jnp.concatenate([panel, nothing] if side == 0 else [nothing, panel], axis=0)

    for side in range(2):
        panel_t[side] = padded_panel(side).T.astype(jnp.bfloat16)
    panel16 = padded_panel(0)[:rank].astype(jnp.bfloat16)

    mine[pl.ds(0, half), :] = jnp.dot(
        panel16[:half], panel_t[0], preferred_element_type=jnp.float32
    ) + jnp.dot(panel16[half:], panel_t[1], preferred_element_type=jnp.float32)

    def part(index):
        return pl.ds(pl.multiple_of(index * size, size), size)

    def right_copy(index, at):
        return pltpu.make_async_remote_copy(
            src_ref=to_right.at[at],
            dst_ref=from_left.at[at],
            send_sem=right_send,
            recv_sem=left_recv.at[index],
            device_id={"cols": lax.rem(col + 1, cols_n)},
            device_id_type=MESH,
        )

    def left_copy(index, at):
        return pltpu.make_async_remote_copy(
            src_ref=to_left.at[at],
            dst_ref=from_right.at[at],
            send_sem=left_send,
            recv_sem=right_recv.at[index],
            device_id={"cols": lax.rem(col + cols_n - 1, cols_n)},
            device_id_type=MESH,
        )

    parts = chunks + 1
    hops = (cols_n - 1) * LAG
    solve_from = hops + 1
    solve_turns = rank // SOLVE_STEPS
    weigh_from = solve_from + solve_turns
    turns = parts + hops
    assert turns - 1 - STRIDE * (chunks // BLOCK_PARTS - 1) >= weigh_from
    lanes = lax.broadcasted_iota(jnp.int32, (rank, 2 * rank), 1)
    sublanes = lax.broadcasted_iota(jnp.int32, (rank, 2 * rank), 0)

    def eliminate(step, _):
        now = system[0:rank, :]
        picked = system[pl.ds(step, 1), :]
        on_lane = lanes == step
        on_row = sublanes == step
        column = jnp.sum(jnp.where(on_lane, now, 0.0), axis=1, keepdims=True)
        pivot = jnp.sum(jnp.where(on_lane[0:1], picked, 0.0), axis=1, keepdims=True)
        new_row = jnp.where(on_lane[0:1], 1.0, picked) / pivot
        rest = jnp.where(on_lane, 0.0, now) - column * new_row
        system[0:rank, :] = jnp.where(on_row, jnp.broadcast_to(new_row, now.shape), rest)
        return 0

    block = BLOCK_PARTS * size
    blocks = chunks // BLOCK_PARTS

    def block_rows(index):
        start = pl.multiple_of(index * block, block)
        return pl.ds(start, block), pl.ds(pl.multiple_of(start + size, size), block)

    def multiply(index):
        at, kept = block_rows(index)
        mine[kept, :] = jnp.dot(
            emb[0, at, :], panel_t[0], preferred_element_type=jnp.float32
        ) + jnp.dot(emb[1, at, :], panel_t[1], preferred_element_type=jnp.float32)

    def block_sum(kept):
        return mine[kept, :] + from_left[kept, :] + from_right[kept, :]

    def weigh(index):
        at, kept = block_rows(index)
        weights_ref[at, :] = jnp.dot(
            block_sum(kept), system[...], precision=HIGH, preferred_element_type=jnp.float32
        )

    gram_at = pl.ds(0, half)

    def pass_right(index, at):
        @pl.when(has_left)
        def _():
            right_copy(index, at).wait_recv()

        @pl.when(has_right)
        def _():
            to_right[at, :] = mine[at, :] + from_left[at, :]
            right_copy(index, at).start()

    def pass_left(index, at):
        @pl.when(has_right)
        def _():
            left_copy(index, at).wait_recv()

        @pl.when(has_left)
        def _():
            to_left[at, :] = mine[at, :] + from_right[at, :]
            left_copy(index, at).start()

    def turn(index, _):
        left_index = index - col * LAG
        right_index = index - (cols_n - 1 - col) * LAG

        @pl.when(left_index == 0)
        def _():
            pass_right(left_index, gram_at)

        @pl.when((left_index >= 1) & (left_index < parts))
        def _():
            pass_right(left_index, part(left_index))

        @pl.when(right_index == 0)
        def _():
            pass_left(right_index, gram_at)

        @pl.when((right_index >= 1) & (right_index < parts))
        def _():
            pass_left(right_index, part(right_index))

        @pl.when((index % BLOCK_PARTS == 0) & (index < chunks))
        def _():
            multiply(index // BLOCK_PARTS)

        @pl.when(index == 2)
        def _():
            for side in range(2):
                padded = padded_panel(side).astype(jnp.bfloat16)
                for piece in range(3):
                    panels_ref[side, pl.ds(piece * 2 * rank, 2 * rank), :] = padded

        @pl.when(index == hops)
        def _():
            at = pl.ds(0, half)
            packed = mine[at, :] + from_left[at, :] + from_right[at, :]
            inside = lanes[0:half] < rank
            system[0:half, :] = jnp.where(inside, packed, 0.0)
            system[half:rank, :] = jnp.where(inside, pltpu.roll(packed, rank, 1), 0.0)

        @pl.when((index >= solve_from) & (index < weigh_from))
        def _():
            lax.fori_loop(
                (index - solve_from) * SOLVE_STEPS,
                (index - solve_from + 1) * SOLVE_STEPS,
                eliminate,
                0,
            )

        @pl.when(index == weigh_from)
        def _():
            system[rank : 2 * rank, :] = pltpu.roll(system[0:rank, :], rank, 1)

        since = index - (turns - 1 - STRIDE * (blocks - 1))

        @pl.when((since >= 0) & (since % STRIDE == STRIDE // 2) & (since < STRIDE * EARLY_BLOCKS))
        def _():
            at, _ = block_rows(since // STRIDE)
            for side in range(2):
                early_ref[side, at, :] = residual_rows(
                    emb[side, at, :], weights_ref[at, :], panels_ref[side]
                )

        @pl.when((since >= 0) & (since % STRIDE == 0) & (since < STRIDE * (blocks - LATE_WEIGHED)))
        def _():
            weigh(since // STRIDE)

        return 0

    lax.fori_loop(0, turns, turn, 0)
    for index in range(blocks - LATE_WEIGHED, blocks):
        at, kept = block_rows(index)
        weights_ref[at, :] = block_sum(kept)

    for step in range(1, rows_n):
        row_copy(step).wait_send()

    def wait_sent(index, at):
        @pl.when(has_right)
        def _():
            right_copy(index, at).wait_send()

        @pl.when(has_left)
        def _():
            left_copy(index, at).wait_send()

    wait_sent(0, pl.ds(size - half, chunks * size + half))


def all_weights(emb3, own, rows_n, cols_n, rank):
    _, pairs, width = emb3.shape
    size = pairs // CHUNKS
    buffer = pltpu.VMEM((pairs + size, 2 * rank), jnp.float32)
    dma = pltpu.SemaphoreType.DMA
    return pl.pallas_call(
        functools.partial(weights_kernel, rows_n, cols_n, CHUNKS),
        out_shape=(
            jax.ShapeDtypeStruct((pairs, 2 * rank), jnp.float32),
            jax.ShapeDtypeStruct((2, 6 * rank, width), jnp.bfloat16),
            jax.ShapeDtypeStruct((2, EARLY_BLOCKS * BLOCK_PARTS * size, width), jnp.float32),
            jax.ShapeDtypeStruct((2 * rank, 2 * rank), jnp.float32),
        ),
        in_specs=[pl.BlockSpec(memory_space=pltpu.VMEM)] * 2,
        out_specs=(pl.BlockSpec(memory_space=pltpu.VMEM),) * 4,
        scratch_shapes=[
            pltpu.VMEM((rows_n,) + own.shape, jnp.float32),
            pltpu.VMEM((2, width, 2 * rank), jnp.bfloat16),
            buffer, buffer, buffer, buffer, buffer,
            dma((rows_n,)), dma((rows_n,)),
            dma, dma((CHUNKS + 1,)), dma, dma((CHUNKS + 1,)),
        ],
        compiler_params=pltpu.CompilerParams(
            collective_id=0, has_side_effects=True, vmem_limit_bytes=16 * MIB
        ),
        cost_estimate=pl.CostEstimate(
            flops=8 * pairs * width * rank, bytes_accessed=2 * emb3.size, transcendentals=0
        ),
    )(emb3, own)


def last_kernel(
    block, emb_ref, weights_ref, panels_ref, early_ref, system_ref, out_ref,
    emb, late, emb_sem, early_sems, late_sems,
):
    early = early_ref.shape[1] // block
    late_count = late.shape[1] // block
    load = pltpu.make_async_copy(emb_ref.at[:, pl.ds(early * block, late_count * block), :], emb, emb_sem)
    load.start()
    copies = []
    for index in range(early):
        at = pl.ds(index * block, block)
        for side in range(2):
            copies.append(
                pltpu.make_async_copy(
                    early_ref.at[side, at], out_ref.at[side, at], early_sems.at[index, side]
                )
            )
            copies[-1].start()
    load.wait()
    for index in range(late_count):
        here = pl.ds(index * block, block)
        at = pl.ds((early + index) * block, block)
        weights = weights_ref[at, :]
        if index >= late_count - LATE_WEIGHED:
            weights = jnp.dot(
                weights, system_ref[...], precision=HIGH, preferred_element_type=jnp.float32
            )
        for side in range(2):
            late[side, here, :] = residual_rows(emb[side, here, :], weights, panels_ref[side])
            copies.append(
                pltpu.make_async_copy(
                    late.at[side, here], out_ref.at[side, at], late_sems.at[index, side]
                )
            )
            copies[-1].start()
    for copy in copies:
        copy.wait()


def last_rows(emb3, weights, panels, early, system):
    _, pairs, width = emb3.shape
    block = BLOCK_PARTS * (pairs // CHUNKS)
    late = pairs - early.shape[1]
    dma = pltpu.SemaphoreType.DMA
    anywhere = pl.BlockSpec(memory_space=pl.ANY)
    inside = pl.BlockSpec(memory_space=pltpu.VMEM)
    return pl.pallas_call(
        functools.partial(last_kernel, block),
        out_shape=jax.ShapeDtypeStruct(emb3.shape, jnp.float32),
        in_specs=[anywhere, inside, inside, anywhere, inside],
        out_specs=anywhere,
        scratch_shapes=[
            pltpu.VMEM((2, late, width), emb3.dtype),
            pltpu.VMEM((2, late, width), jnp.float32),
            dma, dma((early.shape[1] // block, 2)), dma((late // block, 2)),
        ],
        compiler_params=pltpu.CompilerParams(vmem_limit_bytes=16 * MIB),
    )(emb3, weights, panels, early, system)


def per_device(rows_n, cols_n, embeddings, pick_rows):
    row_count, width = embeddings.shape
    rank = pick_rows.shape[0] * pick_rows.shape[1]
    own = own_picks(embeddings, pick_rows, rank // rows_n)
    emb3 = embeddings.reshape(2, row_count // 2, width)
    parts = all_weights(emb3, own, rows_n, cols_n, rank)
    return last_rows(emb3, *parts).reshape(row_count, width)


def solution(mesh):
    in_specs = (P("rows", "cols"), P())
    out_specs = P("rows", "cols")
    return jax.shard_map(
        functools.partial(per_device, mesh.shape["rows"], mesh.shape["cols"]),
        mesh=mesh, in_specs=in_specs, out_specs=out_specs, check_vma=False,
    )
```

```python
import functools

import jax
import jax.numpy as jnp
from jax import lax
from jax.experimental import pallas as pl
from jax.experimental.pallas import tpu as pltpu
from jax.sharding import PartitionSpec as P

HIGH = lax.Precision.HIGHEST
MESH = pl.DeviceIdType.MESH
GROUP = 16
CHUNKS = 32
LAG = 3
BLOCK_PARTS = 4
STRIDE = 2
EARLY_BLOCKS = 5
LATE_WEIGHED = 2
SOLVE_STEPS = 4
MIB = 1024 * 1024


def own_picks_kernel(own_count, picks_ref, emb_ref, out_ref, groups, offsets, sems):
    row_count = emb_ref.shape[0]
    rounds, per_round = picks_ref.shape
    first = lax.axis_index("rows") * row_count

    def look(index, found):
        local = picks_ref[index // per_round, index % per_round] - first
        owned = (local >= 0) & (local < row_count) & (found < own_count)

        @pl.when(owned)
        def _():
            start = pl.multiple_of((local // GROUP) * GROUP, GROUP)
            offsets[found] = local - start
            pltpu.make_async_copy(
                emb_ref.at[pl.ds(start, GROUP), :], groups.at[found], sems.at[found]
            ).start()

        return found + owned.astype(jnp.int32)

    lax.fori_loop(0, rounds * per_round, look, jnp.int32(0), unroll=8)
    for slot in range(own_count):
        pltpu.make_async_copy(
            emb_ref.at[pl.ds(0, GROUP), :], groups.at[slot], sems.at[slot]
        ).wait()
        rows = groups[slot].astype(jnp.float32)
        inside = lax.broadcasted_iota(jnp.int32, rows.shape, 0) == offsets[slot]
        out_ref[pl.ds(slot, 1), :] = jnp.sum(jnp.where(inside, rows, 0.0), axis=0, keepdims=True)


def own_picks(embeddings, picks, own_count):
    width = embeddings.shape[1]
    return pl.pallas_call(
        functools.partial(own_picks_kernel, own_count),
        out_shape=jax.ShapeDtypeStruct((own_count, width), jnp.float32),
        in_specs=[
            pl.BlockSpec(memory_space=pltpu.SMEM),
            pl.BlockSpec(memory_space=pl.ANY),
        ],
        out_specs=pl.BlockSpec(memory_space=pltpu.VMEM),
        scratch_shapes=[
            pltpu.VMEM((own_count, GROUP, width), embeddings.dtype),
            pltpu.SMEM((own_count,), jnp.int32),
            pltpu.SemaphoreType.DMA((own_count,)),
        ],
        compiler_params=pltpu.CompilerParams(vmem_limit_bytes=52 * MIB),
    )(picks, embeddings)


def residual_rows(emb, weights, panel):
    first = weights.astype(jnp.bfloat16)
    rest = weights - first.astype(jnp.float32)
    second = rest.astype(jnp.bfloat16)
    third = (rest - second.astype(jnp.float32)).astype(jnp.bfloat16)
    pieces = jnp.concatenate([first, second, third], axis=1)
    return emb.astype(jnp.float32) - jnp.dot(pieces, panel, preferred_element_type=jnp.float32)


def weights_kernel(
    rows_n, cols_n, chunks, emb, own_ref, weights_ref, panels_ref, early_ref, system,
    gathered, panel_t, mine, from_left, from_right, to_right, to_left,
    row_send, row_recv, right_send, left_recv, left_send, right_recv,
):
    own_count, width = own_ref.shape
    rank = rows_n * own_count
    half = rank // 2
    size = weights_ref.shape[0] // chunks
    row = lax.axis_index("rows")
    col = lax.axis_index("cols")
    has_left = col > 0
    has_right = col < cols_n - 1

    barrier = pltpu.get_barrier_semaphore()
    for step in range(1, rows_n):
        pl.semaphore_signal(
            barrier, inc=1, device_id={"rows": lax.rem(row + step, rows_n)}, device_id_type=MESH
        )

    @pl.when(has_left)
    def _():
        pl.semaphore_signal(barrier, inc=1, device_id={"cols": col - 1}, device_id_type=MESH)

    @pl.when(has_right)
    def _():
        pl.semaphore_signal(barrier, inc=1, device_id={"cols": col + 1}, device_id_type=MESH)

    @pl.when(jnp.logical_not(has_left))
    def _():
        from_left[...] = jnp.zeros_like(from_left)

    @pl.when(jnp.logical_not(has_right))
    def _():
        from_right[...] = jnp.zeros_like(from_right)

    pl.semaphore_wait(
        barrier, rows_n - 1 + has_left.astype(jnp.int32) + has_right.astype(jnp.int32)
    )

    def row_copy(step):
        return pltpu.make_async_remote_copy(
            src_ref=own_ref,
            dst_ref=gathered.at[row],
            send_sem=row_send.at[step],
            recv_sem=row_recv.at[row],
            device_id={"rows": lax.rem(row + step, rows_n)},
            device_id_type=MESH,
        )

    for step in range(1, rows_n):
        row_copy(step).start()
    gathered[row] = own_ref[...]
    for step in range(1, rows_n):
        source = lax.rem(row + step, rows_n)
        pltpu.make_async_remote_copy(
            src_ref=own_ref,
            dst_ref=gathered.at[source],
            send_sem=row_send.at[step],
            recv_sem=row_recv.at[source],
            device_id={"rows": source},
            device_id_type=MESH,
        ).wait_recv()

    def padded_panel(side):
        panel = jnp.concatenate([gathered[owner] for owner in range(rows_n)], axis=0)
        nothing = jnp.zeros_like(panel)
        return jnp.concatenate([panel, nothing] if side == 0 else [nothing, panel], axis=0)

    for side in range(2):
        panel_t[side] = padded_panel(side).T.astype(jnp.bfloat16)
    panel16 = padded_panel(0)[:rank].astype(jnp.bfloat16)

    mine[pl.ds(0, half), :] = jnp.dot(
        panel16[:half], panel_t[0], preferred_element_type=jnp.float32
    ) + jnp.dot(panel16[half:], panel_t[1], preferred_element_type=jnp.float32)

    def part(index):
        return pl.ds(pl.multiple_of(index * size, size), size)

    def right_copy(index, at):
        return pltpu.make_async_remote_copy(
            src_ref=to_right.at[at],
            dst_ref=from_left.at[at],
            send_sem=right_send,
            recv_sem=left_recv.at[index],
            device_id={"cols": lax.rem(col + 1, cols_n)},
            device_id_type=MESH,
        )

    def left_copy(index, at):
        return pltpu.make_async_remote_copy(
            src_ref=to_left.at[at],
            dst_ref=from_right.at[at],
            send_sem=left_send,
            recv_sem=right_recv.at[index],
            device_id={"cols": lax.rem(col + cols_n - 1, cols_n)},
            device_id_type=MESH,
        )

    parts = chunks + 1
    hops = (cols_n - 1) * LAG
    solve_from = hops + 1
    solve_turns = rank // SOLVE_STEPS
    weigh_from = solve_from + solve_turns
    turns = parts + hops
    assert turns - 1 - STRIDE * (chunks // BLOCK_PARTS - 1) >= weigh_from
    lanes = lax.broadcasted_iota(jnp.int32, (rank, 2 * rank), 1)
    sublanes = lax.broadcasted_iota(jnp.int32, (rank, 2 * rank), 0)

    def eliminate(step, _):
        now = system[0:rank, :]
        picked = system[pl.ds(step, 1), :]
        on_lane = lanes == step
        on_row = sublanes == step
        column = jnp.sum(jnp.where(on_lane, now, 0.0), axis=1, keepdims=True)
        pivot = jnp.sum(jnp.where(on_lane[0:1], picked, 0.0), axis=1, keepdims=True)
        new_row = jnp.where(on_lane[0:1], 1.0, picked) / pivot
        rest = jnp.where(on_lane, 0.0, now) - column * new_row
        system[0:rank, :] = jnp.where(on_row, jnp.broadcast_to(new_row, now.shape), rest)
        return 0

    block = BLOCK_PARTS * size
    blocks = chunks // BLOCK_PARTS

    def block_rows(index):
        start = pl.multiple_of(index * block, block)
        return pl.ds(start, block), pl.ds(pl.multiple_of(start + size, size), block)

    def multiply(index):
        at, kept = block_rows(index)
        mine[kept, :] = jnp.dot(
            emb[0, at, :], panel_t[0], preferred_element_type=jnp.float32
        ) + jnp.dot(emb[1, at, :], panel_t[1], preferred_element_type=jnp.float32)

    def block_sum(kept):
        return mine[kept, :] + from_left[kept, :] + from_right[kept, :]

    def weigh(index):
        at, kept = block_rows(index)
        weights_ref[at, :] = jnp.dot(
            block_sum(kept), system[...], precision=HIGH, preferred_element_type=jnp.float32
        )

    gram_at = pl.ds(0, half)

    def pass_right(index, at):
        @pl.when(has_left)
        def _():
            right_copy(index, at).wait_recv()

        @pl.when(has_right)
        def _():
            to_right[at, :] = mine[at, :] + from_left[at, :]
            right_copy(index, at).start()

    def pass_left(index, at):
        @pl.when(has_right)
        def _():
            left_copy(index, at).wait_recv()

        @pl.when(has_left)
        def _():
            to_left[at, :] = mine[at, :] + from_right[at, :]
            left_copy(index, at).start()

    def turn(index, _):
        left_index = index - col * LAG
        right_index = index - (cols_n - 1 - col) * LAG

        @pl.when(left_index == 0)
        def _():
            pass_right(left_index, gram_at)

        @pl.when((left_index >= 1) & (left_index < parts))
        def _():
            pass_right(left_index, part(left_index))

        @pl.when(right_index == 0)
        def _():
            pass_left(right_index, gram_at)

        @pl.when((right_index >= 1) & (right_index < parts))
        def _():
            pass_left(right_index, part(right_index))

        @pl.when((index % BLOCK_PARTS == 0) & (index < chunks))
        def _():
            multiply(index // BLOCK_PARTS)

        @pl.when(index == 2)
        def _():
            for side in range(2):
                padded = padded_panel(side).astype(jnp.bfloat16)
                for piece in range(3):
                    panels_ref[side, pl.ds(piece * 2 * rank, 2 * rank), :] = padded

        @pl.when(index == hops)
        def _():
            at = pl.ds(0, half)
            packed = mine[at, :] + from_left[at, :] + from_right[at, :]
            inside = lanes[0:half] < rank
            system[0:half, :] = jnp.where(inside, packed, 0.0)
            system[half:rank, :] = jnp.where(inside, pltpu.roll(packed, rank, 1), 0.0)

        @pl.when((index >= solve_from) & (index < weigh_from))
        def _():
            lax.fori_loop(
                (index - solve_from) * SOLVE_STEPS,
                (index - solve_from + 1) * SOLVE_STEPS,
                eliminate,
                0,
            )

        @pl.when(index == weigh_from)
        def _():
            system[rank : 2 * rank, :] = pltpu.roll(system[0:rank, :], rank, 1)

        since = index - (turns - 1 - STRIDE * (blocks - 1))

        @pl.when((since >= 0) & (since % STRIDE == STRIDE // 2) & (since < STRIDE * EARLY_BLOCKS))
        def _():
            at, _ = block_rows(since // STRIDE)
            for side in range(2):
                early_ref[side, at, :] = residual_rows(
                    emb[side, at, :], weights_ref[at, :], panels_ref[side]
                )

        @pl.when((since >= 0) & (since % STRIDE == 0) & (since < STRIDE * (blocks - LATE_WEIGHED)))
        def _():
            weigh(since // STRIDE)

        return 0

    lax.fori_loop(0, turns, turn, 0)
    for index in range(blocks - LATE_WEIGHED, blocks):
        at, kept = block_rows(index)
        weights_ref[at, :] = block_sum(kept)

    for step in range(1, rows_n):
        row_copy(step).wait_send()

    def wait_sent(index, at):
        @pl.when(has_right)
        def _():
            right_copy(index, at).wait_send()

        @pl.when(has_left)
        def _():
            left_copy(index, at).wait_send()

    wait_sent(0, pl.ds(size - half, chunks * size + half))


def all_weights(emb3, own, rows_n, cols_n, rank):
    _, pairs, width = emb3.shape
    size = pairs // CHUNKS
    buffer = pltpu.VMEM((pairs + size, 2 * rank), jnp.float32)
    dma = pltpu.SemaphoreType.DMA
    return pl.pallas_call(
        functools.partial(weights_kernel, rows_n, cols_n, CHUNKS),
        out_shape=(
            jax.ShapeDtypeStruct((pairs, 2 * rank), jnp.float32),
            jax.ShapeDtypeStruct((2, 6 * rank, width), jnp.bfloat16),
            jax.ShapeDtypeStruct((2, EARLY_BLOCKS * BLOCK_PARTS * size, width), jnp.float32),
            jax.ShapeDtypeStruct((2 * rank, 2 * rank), jnp.float32),
        ),
        in_specs=[pl.BlockSpec(memory_space=pltpu.VMEM)] * 2,
        out_specs=(pl.BlockSpec(memory_space=pltpu.VMEM),) * 4,
        scratch_shapes=[
            pltpu.VMEM((rows_n,) + own.shape, jnp.float32),
            pltpu.VMEM((2, width, 2 * rank), jnp.bfloat16),
            buffer, buffer, buffer, buffer, buffer,
            dma((rows_n,)), dma((rows_n,)),
            dma, dma((CHUNKS + 1,)), dma, dma((CHUNKS + 1,)),
        ],
        compiler_params=pltpu.CompilerParams(
            collective_id=0, has_side_effects=True, vmem_limit_bytes=16 * MIB
        ),
        cost_estimate=pl.CostEstimate(
            flops=8 * pairs * width * rank, bytes_accessed=2 * emb3.size, transcendentals=0
        ),
    )(emb3, own)


def last_kernel(
    block, emb_ref, weights_ref, panels_ref, early_ref, system_ref, out_ref,
    emb, late, emb_sem, early_sems, late_sems,
):
    early = early_ref.shape[1] // block
    late_count = late.shape[1] // block
    load = pltpu.make_async_copy(emb_ref.at[:, pl.ds(early * block, late_count * block), :], emb, emb_sem)
    load.start()
    copies = []
    for index in range(early):
        at = pl.ds(index * block, block)
        for side in range(2):
            copies.append(
                pltpu.make_async_copy(
                    early_ref.at[side, at], out_ref.at[side, at], early_sems.at[index, side]
                )
            )
            copies[-1].start()
    load.wait()
    for index in range(late_count):
        here = pl.ds(index * block, block)
        at = pl.ds((early + index) * block, block)
        weights = weights_ref[at, :]
        if index >= late_count - LATE_WEIGHED:
            weights = jnp.dot(
                weights, system_ref[...], precision=HIGH, preferred_element_type=jnp.float32
            )
        for side in range(2):
            late[side, here, :] = residual_rows(emb[side, here, :], weights, panels_ref[side])
            copies.append(
                pltpu.make_async_copy(
                    late.at[side, here], out_ref.at[side, at], late_sems.at[index, side]
                )
            )
            copies[-1].start()
    for copy in copies:
        copy.wait()


def last_rows(emb3, weights, panels, early, system):
    _, pairs, width = emb3.shape
    block = BLOCK_PARTS * (pairs // CHUNKS)
    late = pairs - early.shape[1]
    dma = pltpu.SemaphoreType.DMA
    anywhere = pl.BlockSpec(memory_space=pl.ANY)
    inside = pl.BlockSpec(memory_space=pltpu.VMEM)
    return pl.pallas_call(
        functools.partial(last_kernel, block),
        out_shape=jax.ShapeDtypeStruct(emb3.shape, jnp.float32),
        in_specs=[anywhere, inside, inside, anywhere, inside],
        out_specs=anywhere,
        scratch_shapes=[
            pltpu.VMEM((2, late, width), emb3.dtype),
            pltpu.VMEM((2, late, width), jnp.float32),
            dma, dma((early.shape[1] // block, 2)), dma((late // block, 2)),
        ],
        compiler_params=pltpu.CompilerParams(vmem_limit_bytes=16 * MIB),
    )(emb3, weights, panels, early, system)


def per_device(rows_n, cols_n, embeddings, pick_rows):
    row_count, width = embeddings.shape
    rank = pick_rows.shape[0] * pick_rows.shape[1]
    own = own_picks(embeddings, pick_rows, rank // rows_n)
    emb3 = embeddings.reshape(2, row_count // 2, width)
    parts = all_weights(emb3, own, rows_n, cols_n, rank)
    return last_rows(emb3, *parts).reshape(row_count, width)


def solution(mesh):
    in_specs = (P("rows", "cols"), P())
    out_specs = P("rows", "cols")
    return jax.shard_map(
        functools.partial(per_device, mesh.shape["rows"], mesh.shape["cols"]),
        mesh=mesh, in_specs=in_specs, out_specs=out_specs, check_vma=False,
    )
```
